512 devices in a mesh: dp: 8 (over x, core), ctx: 8 (over z), tp: 8 (over y).
Axes of the slice: x: 4, y: 8, z: 8, core: 2. Of those that a mesh axis runs over, the one named last changes fastest.
Arguments:
- tokens: bfloat16 [4096, 4096], P(('dp', 'ctx', 'tp')), may hold values from -6 to 6
- routes: int32 [4096, 2], P(('dp', 'ctx', 'tp')), may hold values from 0 to 63, all different within a row; in each aligned block of 64 rows (0 to 63, 64 to 127, ...) at most 2 rows name the same one
- gate_weights: float32 [4096, 2], P(('dp', 'ctx', 'tp')), may hold values from 0.2 to 1
- seq_ids: int32 [4096], P(('dp', 'ctx', 'tp')), may hold values from 0 to 127, never falling along the last dimension, each value on 1 to 64 neighbouring positions
- log_ratio: float32 [4096], P(('dp', 'ctx', 'tp')), may hold values from -0.5 to 0.9
- advantage: float32 [128], replicated, may hold values from -4 to 4
- upstream: bfloat16 [4096, 4096], P(('dp', 'ctx', 'tp')), may hold values from -6 to 6
- w_gate: bfloat16 [64, 4096, 1024], P(('dp', 'ctx'), None, 'tp'), may hold values from -0.09375 to 0.09375
- w_up: bfloat16 [64, 4096, 1024], P(('dp', 'ctx'), None, 'tp'), may hold values from -0.09375 to 0.09375
- w_down: bfloat16 [64, 1024, 4096], P(('dp', 'ctx'), 'tp'), may hold values from -0.1875 to 0.1875
Outputs:
- mixed: bfloat16 [4096, 4096], P(('dp', 'ctx', 'tp'))
- grad_tokens: bfloat16 [4096, 4096], P(('dp', 'ctx', 'tp'))
- grad_gates: float32 [4096, 2], P(('dp', 'ctx', 'tp'))
The draws below stay inside these ranges and needn't reach their ends.
Inputs may be any that keep to these rules, and one draw needn't show every extreme that they name: `routes`: A row's 2 ids differ. In each aligned block of 64 rows no expert is named more than 2 times, a bound that some block reaches. `seq_ids`: never falling; every sequence has 1 to 64 tokens, one exactly 64.
All inputs are finite; a program needn't handle non-finite values.
Results may differ from the reference program's by a relative error of at most 0.025.
Values may be sent and summed in bfloat16 or wider, within the bound.
No kernel may reach another device: no remote copies, remote signals or barrier semaphores. Data moves between devices by JAX's collectives and lax.ppermute only.
A program may use at most 64 MiB of HBM per device.

```python
import math
import jax
import jax.numpy as jnp
import numpy as np
from jax import lax

D = 4096
EFF = 1024
TOPK = 2
TOK_DEV = 8
EXPERTS = 64
TOKENS = 4096
CAP = 2
NSEQ = 128
SEQ_MOST = 64
N_DP = 8
N_CTX = 8
N_TP = 8


def level_of(rng, shape, cuts, low, largest):
    factor_of, own = 1.0, jax.random.fold_in(rng, 6)
    for dim, blocks in cuts:
        heights = jnp.exp(jax.random.uniform(jax.random.fold_in(own, dim), (blocks,), jnp.float32, low / len(cuts), largest / len(cuts)))
        factor_of = factor_of * jnp.repeat(heights, shape[dim] // blocks).reshape([-1 if axis == dim else 1 for axis in range(len(shape))])
    return factor_of


def split_up(amount, total, most, skew):
    loads = [(1 << 20) // math.isqrt(rank ** skew) + 1 for rank in range(2, amount + 1)]
    surplus, given = total - most - (amount - 1), [1] * (amount - 1)
    while surplus > 0:
        free = [i for i in range(amount - 1) if given[i] < most]
        mass, budget = sum([loads[i] for i in free]), surplus
        for i in free:
            addition = min(most - given[i], max(1, budget * loads[i] // mass), surplus)
            given[i] = given[i] + addition
            surplus = surplus - addition
    return np.array([most] + given)


def ragged(own_key, count, total, bound, lean):
    if count == 2:
        one = jax.random.randint(own_key, (), max(1, total - bound), min(bound, total - 1) + 1)
        return jnp.stack([one, total - one])
    tallies = jnp.asarray(split_up(count, total, bound, lean), jnp.int32)
    twos = (count - 1) // 2
    donor, taker = tallies[1:1 + 2 * twos:2], tallies[2:2 + 2 * twos:2]
    slack = jnp.minimum(donor - 1, bound - taker)
    moved = jax.random.randint(jax.random.fold_in(own_key, 1), (twos,), 0, 1 << 20) % (slack + 1)
    tallies = tallies.at[1:1 + 2 * twos:2].set(donor - moved).at[2:2 + 2 * twos:2].set(taker + moved)
    return tallies[jax.random.permutation(jax.random.fold_in(own_key, 2), count)]


def shared_out(stream_key, own, number, rows, amount, top, most, lean):
    order = jax.random.permutation(stream_key, amount)
    crowded, ordinary = load_shares(amount, rows * top, most, lean, True), load_shares(amount, rows * top, most, lean, False)
    places = jnp.arange(amount)

    def named(lengths, turn):
        used = int((lengths > 0).sum())
        fixed = max(1, used // 4)
        shifted = fixed + (places - fixed + turn * (used - fixed)) % max(1, amount - fixed)
        return jnp.zeros((amount,), jnp.int32).at[order[jnp.where(places < fixed, places, shifted)]].set(jnp.asarray(lengths, jnp.int32))

    lengths = jnp.where(number % 4 == 0, named(crowded, number // 4), named(ordinary, number - number // 4 - 1))
    mixed = jax.random.permutation(jax.random.fold_in(own, 3), amount)
    donor, taker = mixed[0:amount // 2 * 2:2], mixed[1:amount // 2 * 2:2]
    margin = jnp.minimum(lengths[donor] - 1, most - lengths[taker]) // 2
    margin = jnp.where((donor == order[0]) | (taker == order[0]) | (lengths[taker] == 0), 0, jnp.maximum(margin, 0))
    shifted = jax.random.randint(jax.random.fold_in(own, 4), (amount // 2,), 0, 1 << 20) % (margin + 1)
    lengths = lengths.at[donor].add(-shifted).at[taker].add(shifted)
    items = jnp.searchsorted(jnp.cumsum(lengths), jnp.arange(rows * top), side="right").astype(jnp.int32)
    grid = items.reshape(top, rows).T
    grid = grid[jax.random.permutation(jax.random.fold_in(own, 1), rows)]
    turn = jax.random.randint(jax.random.fold_in(own, 2), (rows, 1), 0, top)
    return jnp.take_along_axis(grid, (jnp.arange(top)[None, :] + turn) % top, axis=1)


def load_shares(amount, total, limit, slope, full):
    weights = [(1 << 20) // math.isqrt(standing ** slope) + 1 for standing in range(1, amount + 1)]
    largest = limit if full else min(limit, max(-(-total // amount), total * weights[0] // sum(weights)))
    least = 1 if total - largest >= amount - 1 else 0
    holding, spare = [largest] + [least] * (amount - 1), total - largest - least * (amount - 1)
    while spare > 0:
        free = [i for i in range(1, amount) if holding[i] < largest] or [i for i in range(1, amount) if holding[i] < limit]
        mass, remaining = sum([weights[i] for i in free]), spare
        for i in free:
            extra = min(limit - holding[i], max(1, remaining * weights[i] // mass), spare)
            holding[i] = holding[i] + extra
            spare = spare - extra
    return np.array(holding)


def centred(rng, shape, spread, reach, shards=(), held_as=jnp.bfloat16):
    loudness = level_of(rng, shape, shards, -0.22, 0.18) if shards else 1.0
    entries = jax.random.normal(rng, shape, jnp.float32) * spread * loudness
    return jnp.minimum(jnp.maximum(entries, -reach), reach).astype(held_as)


def setup_inputs(seed: int = 0) -> dict:
    arg_keys = jax.random.split(jax.random.key(seed), 11)
    tokens = centred(arg_keys[0], (TOKENS, D), 1.0, 6.0, ((0, 512),))
    routes_keys = jax.random.split(jax.random.fold_in(arg_keys[1], 1), TOKENS // (TOK_DEV * N_TP))
    routes_turns = jax.random.permutation(jax.random.fold_in(arg_keys[1], 3), TOKENS // (TOK_DEV * N_TP))
    routes = jax.vmap(lambda own, number: shared_out(jax.random.fold_in(arg_keys[1], 2), own, number, TOK_DEV * N_TP, EXPERTS, TOPK, CAP, 2))(routes_keys, routes_turns).reshape((TOKENS, TOPK))
    gate_weights = jnp.clip(0.2 + 0.8 * jax.random.uniform(arg_keys[2], (TOKENS, TOPK), jnp.float32) ** level_of(arg_keys[2], (TOKENS, TOPK), ((0, 512),), -0.2, 0.2), 0.2, 1.0)
    seq_ids = jnp.searchsorted(jnp.cumsum(ragged(arg_keys[3], NSEQ, TOKENS, SEQ_MOST, 2)), jnp.arange(TOKENS), side="right").astype(jnp.int32)
    log_ratio = jnp.clip(-0.5 + 1.4 * jax.random.uniform(arg_keys[4], (TOKENS,), jnp.float32) ** level_of(arg_keys[4], (TOKENS,), ((0, 512),), -0.2, 0.2), -0.5, 0.9)
    advantage = centred(arg_keys[5], (NSEQ,), 1.0, 4.0, (), jnp.float32)
    upstream = centred(arg_keys[6], (TOKENS, D), 1.0, 6.0, ((0, 512),))
    w_gate = centred(arg_keys[7], (EXPERTS, D, EFF), D ** -0.5, 0.09375, ((0, 64), (2, 8)))
    w_up = centred(arg_keys[8], (EXPERTS, D, EFF), D ** -0.5, 0.09375, ((0, 64), (2, 8)))
    w_down = centred(arg_keys[9], (EXPERTS, EFF, D), EFF ** -0.5, 0.1875, ((0, 64), (1, 8)))
    return {"tokens": tokens, "routes": routes, "gate_weights": gate_weights, "seq_ids": seq_ids, "log_ratio": log_ratio, "advantage": advantage, "upstream": upstream, "w_gate": w_gate, "w_up": w_up, "w_down": w_down}


CLIP_HIGH = 1.2
HIGHEST = lax.Precision.HIGHEST


def expert_pass(operands):
    x_rows, dy_rows, gate_mat, up_mat, down_mat = operands
    hidden_share = EFF // N_TP
    gate_pre = jnp.dot(x_rows, gate_mat, preferred_element_type=jnp.float32)
    up_pre = jnp.dot(x_rows, up_mat, preferred_element_type=jnp.float32)
    squash = jax.nn.sigmoid(gate_pre)
    activated = gate_pre * squash
    hidden = (activated * up_pre).astype(jnp.bfloat16)
    parts = jnp.einsum("rgf,gfd->rgd", hidden.reshape(-1, N_TP, hidden_share).astype(jnp.float32),
                       down_mat.reshape(N_TP, hidden_share, D).astype(jnp.float32)).astype(jnp.bfloat16)
    part_total = jnp.sum(parts.astype(jnp.float32), axis=1)
    gate_terms = jnp.einsum("rgd,rd->rg", parts.astype(jnp.float32), dy_rows.astype(jnp.float32)).astype(jnp.bfloat16)
    gate_terms = lax.optimization_barrier(gate_terms)
    grad_part = jnp.sum(gate_terms.astype(jnp.float32), axis=1)
    d_hidden = lax.dot_general(dy_rows, down_mat, (((1,), (1,)), ((), ())), preferred_element_type=jnp.float32)
    grad_in_gate = (d_hidden * up_pre * squash * (1.0 + gate_pre * (1.0 - squash))).astype(jnp.bfloat16)
    grad_in_up = (d_hidden * activated).astype(jnp.bfloat16)
    contrib = jnp.einsum("rgf,dgf->rgd", grad_in_gate.reshape(-1, N_TP, hidden_share).astype(jnp.float32),
                         gate_mat.reshape(D, N_TP, hidden_share).astype(jnp.float32))
    contrib = contrib + jnp.einsum("rgf,dgf->rgd", grad_in_up.reshape(-1, N_TP, hidden_share).astype(jnp.float32),
                                   up_mat.reshape(D, N_TP, hidden_share).astype(jnp.float32))
    contrib = lax.optimization_barrier(contrib.astype(jnp.bfloat16))
    input_total = jnp.sum(contrib.astype(jnp.float32), axis=1)
    return part_total, input_total, grad_part


def reference(tokens, routes, gate_weights, seq_ids, log_ratio, advantage, upstream, w_gate, w_up, w_down):
    groups = N_DP * N_CTX
    tok_group = TOK_DEV * N_TP
    member = (seq_ids[:, None] == jnp.arange(NSEQ, dtype=jnp.int32)[None, :]).astype(jnp.float32)
    seq_sums = jnp.dot(log_ratio, member, precision=HIGHEST)
    counts = jnp.sum(member, axis=0)
    weight = advantage * jnp.minimum(jnp.exp(seq_sums / counts), CLIP_HIGH)
    token_weight = jnp.dot(member, weight, precision=HIGHEST)
    cotangent = (upstream.astype(jnp.float32) * token_weight[:, None]).astype(jnp.bfloat16)

    flattened = routes.reshape(groups, tok_group * TOPK)
    one_hot = (flattened[:, :, None] == jnp.arange(EXPERTS, dtype=jnp.int32)[None, None, :]).astype(jnp.int32)
    earlier = jnp.cumsum(one_hot, axis=1) - one_hot
    position = jnp.sum(earlier * one_hot, axis=2)
    group_id = jnp.arange(groups, dtype=jnp.int32)[:, None]
    slot_index = (flattened * (groups * CAP) + group_id * CAP + position).reshape(-1).astype(jnp.int32)
    token_ids = (jnp.arange(TOKENS * TOPK, dtype=jnp.int32) // TOPK).astype(jnp.int32)
    buffer_rows = EXPERTS * groups * CAP
    x_slots = jnp.zeros((buffer_rows, D), jnp.bfloat16).at[slot_index].set(tokens[token_ids])
    dy_slots = jnp.zeros((buffer_rows, D), jnp.bfloat16).at[slot_index].set(cotangent[token_ids])
    part_total, input_total, grad_part = lax.map(expert_pass, (
        x_slots.reshape(EXPERTS, groups * CAP, D), dy_slots.reshape(EXPERTS, groups * CAP, D), w_gate, w_up, w_down))
    picked = part_total.reshape(buffer_rows, D)[slot_index].reshape(TOKENS, TOPK, D)
    mixed = jnp.sum(picked * gate_weights[:, :, None], axis=1).astype(jnp.bfloat16)
    picked_grad = input_total.reshape(buffer_rows, D)[slot_index].reshape(TOKENS, TOPK, D)
    grad_tokens = jnp.sum(picked_grad * gate_weights[:, :, None], axis=1).astype(jnp.bfloat16)
    grad_gates = grad_part.reshape(buffer_rows)[slot_index].reshape(TOKENS, TOPK)
    return mixed, grad_tokens, grad_gates
```

```python
import jax
import jax.numpy as jnp
from jax import lax
from jax.experimental import pallas as pl
from jax.experimental.pallas import tpu as pltpu
from jax.sharding import PartitionSpec as P

CLIP_HIGH = 1.2
GROUP_AXES = ("dp", "ctx")
META = 128
F32 = jnp.float32
BF16 = jnp.bfloat16


def split3(value):
    high = value.astype(BF16).astype(F32)
    rest = value - high
    middle = rest.astype(BF16).astype(F32)
    return high, middle, rest - middle


def lanes(rows, columns):
    lane = lax.broadcasted_iota(jnp.int32, (rows, META), 1)
    total = jnp.zeros((rows, META), F32)
    for place, column in enumerate(columns):
        total = total + jnp.where(lane == place, column, 0.0)
    return total


def pack_kernel(tokens, upstream, routes, gates, ids, ratio, out):
    parts, rows = out.shape[0], out.shape[1]
    width = tokens.shape[1] // parts
    gate_parts = split3(gates[...])
    columns = [routes[:, 0:1].astype(F32), routes[:, 1:2].astype(F32), ids[...].astype(F32)]
    columns += list(split3(ratio[...]))
    for k in range(2):
        columns += [piece[:, k : k + 1] for piece in gate_parts]
    meta = lanes(rows, columns).astype(BF16)
    for t in range(parts):
        out[t, :, 0:width] = tokens[:, t * width : (t + 1) * width]
        out[t, :, width : 2 * width] = upstream[:, t * width : (t + 1) * width]
        out[t, :, 2 * width : 2 * width + META] = meta


def slot_one_hots(meta, experts, capacity):
    count = meta.shape[0]
    expert = lax.broadcasted_iota(jnp.int32, (count, experts), 1).astype(F32)
    chosen = [(meta[:, k : k + 1] == expert).astype(F32) for k in range(2)]
    row = lax.broadcasted_iota(jnp.int32, (count, count), 0)
    column = lax.broadcasted_iota(jnp.int32, (count, count), 1)
    before = jnp.dot(
        (column < row).astype(BF16),
        (chosen[0] + chosen[1]).astype(BF16),
        preferred_element_type=F32,
    )
    slot = lax.broadcasted_iota(jnp.int32, (count, experts * capacity), 1).astype(F32)
    result = []
    for k in range(2):
        position = jnp.sum(before * chosen[k], axis=1, keepdims=True)
        result.append((meta[:, k : k + 1] * capacity + position == slot).astype(F32))
    return result


def dispatch_kernel(group, out):
    experts = out.shape[0] // 2
    width = out.shape[1]
    hots = slot_one_hots(group[:, width : width + META].astype(F32), experts, 2)
    out[...] = lax.dot_general(
        (hots[0] + hots[1]).astype(BF16),
        group[:, 0:width],
        (((0,), (0,)), ((), ())),
        preferred_element_type=F32,
    ).astype(BF16)


def expert_kernel(arrived, w_gate, w_up, w_down, out):
    parts = arrived.shape[0]
    width = arrived.shape[2] // 2
    gate_pre = up_pre = d_hidden = 0.0
    for t in range(parts):
        cut = slice(t * width, (t + 1) * width)
        rows = arrived[t, :, 0:width]
        gate_pre += jnp.dot(rows, w_gate[cut, :], preferred_element_type=F32)
        up_pre += jnp.dot(rows, w_up[cut, :], preferred_element_type=F32)
        d_hidden += lax.dot_general(
            arrived[t, :, width : 2 * width],
            w_down[:, cut],
            (((1,), (1,)), ((), ())),
            preferred_element_type=F32,
        )
    squash = jax.nn.sigmoid(gate_pre)
    activated = gate_pre * squash
    hidden = (activated * up_pre).astype(BF16)
    d_gate = (d_hidden * up_pre * squash * (1.0 + gate_pre * (1.0 - squash))).astype(BF16)
    d_up = (d_hidden * activated).astype(BF16)
    for t in range(parts):
        cut = slice(t * width, (t + 1) * width)
        out[t, :, 0:width] = jnp.dot(
            hidden, w_down[:, cut], preferred_element_type=F32
        ).astype(BF16)
        contract = (((1,), (1,)), ((), ()))
        out[t, :, width : 2 * width] = (
            lax.dot_general(d_gate, w_gate[cut, :], contract, preferred_element_type=F32)
            + lax.dot_general(d_up, w_up[cut, :], contract, preferred_element_type=F32)
        ).astype(BF16)


def combine_kernel(back, group, meta_before, meta_after, advantage, out):
    slots, both = back.shape
    width = both // 2
    count = group.shape[0]
    meta = group[:, both : both + META].astype(F32)
    hots = slot_one_hots(meta, slots // 2, 2)
    near = jnp.concatenate(
        [meta_before[...].astype(F32), meta, meta_after[...].astype(F32)], axis=0
    ).T
    same = (meta[:, 2:3] == near[2:3, :]).astype(F32)
    ratio_row = near[3:4, :] + near[4:5, :] + near[5:6, :]
    tally = jnp.sum(same, axis=1, keepdims=True)
    ratio = jnp.exp(jnp.sum(same * ratio_row, axis=1, keepdims=True) / tally)
    sequence = lax.broadcasted_iota(jnp.int32, (count, advantage.shape[1]), 1).astype(F32)
    own = jnp.sum(
        jnp.where(meta[:, 2:3] == sequence, advantage[...], 0.0), axis=1, keepdims=True
    )
    weight = own * jnp.minimum(ratio, CLIP_HIGH)
    upstream = group[:, width:both].astype(F32)
    total = 0.0
    columns = []
    for k in range(2):
        picked = jnp.dot(hots[k].astype(BF16), back[...], preferred_element_type=F32)
        first = 6 + 3 * k
        gate = meta[:, first : first + 1] + meta[:, first + 1 : first + 2]
        gate = gate + meta[:, first + 2 : first + 3]
        total = total + gate * picked
        term = weight * jnp.sum(upstream * picked[:, 0:width], axis=1, keepdims=True)
        columns += list(split3(term))
    out[:, 0:width] = total[:, 0:width].astype(BF16)
    out[:, width:both] = (weight * total[:, width:both]).astype(BF16)
    out[:, both : both + META] = lanes(count, columns).astype(BF16)


def unpack_kernel(arrived, mixed, grad_tokens, grad_gates):
    parts = arrived.shape[0]
    width = mixed.shape[1] // parts
    terms = jnp.zeros((arrived.shape[1], META), F32)
    for t in range(parts):
        cut = slice(t * width, (t + 1) * width)
        mixed[:, cut] = arrived[t, :, 0:width]
        grad_tokens[:, cut] = arrived[t, :, width : 2 * width]
        terms += arrived[t, :, 2 * width : 2 * width + META].astype(F32)
    for k in range(2):
        grad_gates[:, k : k + 1] = (
            terms[:, 3 * k : 3 * k + 1]
            + terms[:, 3 * k + 1 : 3 * k + 2]
            + terms[:, 3 * k + 2 : 3 * k + 3]
        )


def call(kernel, shapes, *operands):
    return pl.pallas_call(
        kernel,
        out_shape=shapes,
        compiler_params=pltpu.CompilerParams(vmem_limit_bytes=32 * 1024 * 1024),
    )(*operands)


def struct(*shape, dtype=BF16):
    return jax.ShapeDtypeStruct(shape, dtype)


def per_device(
    tokens, routes, gate_weights, seq_ids, log_ratio, advantage, upstream, w_gate, w_up, w_down
):
    count, model = tokens.shape
    parts = lax.axis_size("tp")
    groups = lax.axis_size("dp") * lax.axis_size("ctx")
    group_tokens = count * parts
    width = model // parts
    slots = 2 * groups

    packed = call(
        pack_kernel,
        struct(parts, count, 2 * width + META),
        tokens,
        upstream,
        routes,
        gate_weights,
        seq_ids.reshape(count, 1),
        log_ratio.reshape(count, 1),
    )
    group = lax.all_to_all(packed, "tp", 0, 0).reshape(group_tokens, 2 * width + META)
    sent = call(dispatch_kernel, struct(slots, 2 * width), group)
    slot_rows = lax.all_to_all(sent.reshape(groups, 2, 2 * width), GROUP_AXES, 0, 0)
    arrived = lax.all_gather(slot_rows.reshape(slots, 2 * width), "tp")

    meta = group[:, 2 * width :]
    meta_before = lax.ppermute(meta, GROUP_AXES, [(i, (i + 1) % groups) for i in range(groups)])
    meta_after = lax.ppermute(meta, GROUP_AXES, [((i + 1) % groups, i) for i in range(groups)])

    results = call(
        expert_kernel, struct(parts, slots, 2 * width), arrived, w_gate[0], w_up[0], w_down[0]
    )
    summed = lax.psum_scatter(results, "tp")
    back = lax.all_to_all(summed.reshape(groups, 2, 2 * width), GROUP_AXES, 0, 0)
    combined = call(
        combine_kernel,
        struct(group_tokens, 2 * width + META),
        back.reshape(slots, 2 * width),
        group,
        meta_before,
        meta_after,
        advantage.reshape(1, -1),
    )
    home = lax.all_to_all(combined.reshape(parts, count, 2 * width + META), "tp", 0, 0)
    return call(
        unpack_kernel,
        (struct(count, model), struct(count, model), struct(count, 2, dtype=F32)),
        home,
    )


def solution(mesh):
    rows = ("dp", "ctx", "tp")
    in_specs = (
        P(rows, None),
        P(rows, None),
        P(rows, None),
        P(rows),
        P(rows),
        P(),
        P(rows, None),
        P(GROUP_AXES, None, "tp"),
        P(GROUP_AXES, None, "tp"),
        P(GROUP_AXES, "tp", None),
    )
    out_specs = (P(rows, None), P(rows, None), P(rows, None))
    return jax.shard_map(
        per_device, mesh=mesh, in_specs=in_specs, out_specs=out_specs, check_vma=False
    )
```

```python
import jax
import jax.numpy as jnp
from jax import lax
from jax.experimental import pallas as pl
from jax.experimental.pallas import tpu as pltpu
from jax.sharding import PartitionSpec as P

CLIP_HIGH = 1.2
GROUP_AXES = ("dp", "ctx")
META = 128
CUTS = 4
F32 = jnp.float32
BF16 = jnp.bfloat16


def split3(value):
    high = value.astype(BF16).astype(F32)
    rest = value - high
    middle = rest.astype(BF16).astype(F32)
    return high, middle, rest - middle


def columns_of(rows_by_one, count):
    eye = lax.broadcasted_iota(jnp.int32, (count, count), 0) == lax.broadcasted_iota(
        jnp.int32, (count, count), 1
    )
    return jnp.sum(jnp.where(eye, rows_by_one, 0.0), axis=1, keepdims=True)


def row_of(column, count):
    eye = lax.broadcasted_iota(jnp.int32, (count, count), 0) == lax.broadcasted_iota(
        jnp.int32, (count, count), 1
    )
    return jnp.sum(jnp.where(eye, column, 0.0), axis=0, keepdims=True)


def lanes(rows, columns):
    lane = lax.broadcasted_iota(jnp.int32, (rows, META), 1)
    total = jnp.zeros((rows, META), F32)
    for place, column in enumerate(columns):
        total = total + jnp.where(lane == place, column, 0.0)
    return total


def pack_kernel(tokens, upstream, routes, gates, ids, ratio, out):
    parts, rows = out.shape[0], out.shape[1]
    width = tokens.shape[1] // CUTS
    rows_in = [routes[0:1, :].astype(F32), routes[1:2, :].astype(F32), ids[...].astype(F32)]
    rows_in += list(split3(ratio[...]))
    gate_parts = split3(gates[...])
    for k in range(2):
        rows_in += [piece[k : k + 1, :] for piece in gate_parts]
    meta = lanes(rows, [columns_of(row, rows) for row in rows_in]).astype(BF16)
    for t in range(parts):
        cut = slice((t % CUTS) * width, (t % CUTS + 1) * width)
        out[t, :, 0:width] = tokens[:, cut]
        out[t, :, width : 2 * width] = upstream[:, cut]
        out[t, :, 2 * width : 2 * width + META] = meta


def slot_one_hots(meta, experts, capacity):
    count = meta.shape[0]
    expert = lax.broadcasted_iota(jnp.int32, (count, experts), 1).astype(F32)
    chosen = [(meta[:, k : k + 1] == expert).astype(F32) for k in range(2)]
    row = lax.broadcasted_iota(jnp.int32, (count, count), 0)
    column = lax.broadcasted_iota(jnp.int32, (count, count), 1)
    before = jnp.dot(
        (column < row).astype(BF16),
        (chosen[0] + chosen[1]).astype(BF16),
        preferred_element_type=F32,
    )
    slot = lax.broadcasted_iota(jnp.int32, (count, experts * capacity), 1).astype(F32)
    result = []
    for k in range(2):
        position = jnp.sum(before * chosen[k], axis=1, keepdims=True)
        result.append((meta[:, k : k + 1] * capacity + position == slot).astype(F32))
    return result


def dispatch_kernel(group, out):
    slots = out.shape[0]
    width = out.shape[1] - META
    meta = group[:, width : width + META].astype(F32)
    hots = slot_one_hots(meta, slots // 2, 2)
    out[:, 0:width] = lax.dot_general(
        (hots[0] + hots[1]).astype(BF16),
        group[:, 0:width],
        (((0,), (0,)), ((), ())),
        preferred_element_type=F32,
    ).astype(BF16)
    across = meta.T
    first = jnp.concatenate([across[2:3, :], across[3:4, :]], axis=1)
    second = jnp.concatenate([across[4:5, :], across[5:6, :]], axis=1)
    odd = lax.broadcasted_iota(jnp.int32, (slots, META), 0) % 2 == 1
    out[:, width : width + META] = jnp.where(odd, second, first).astype(BF16)


def weight_kernel(near, group, advantage, out):
    groups = near.shape[0] // 2
    count = group.shape[0]
    here = lax.axis_index("dp") * lax.axis_size("ctx") + lax.axis_index("ctx")
    wanted = lax.broadcasted_iota(jnp.int32, (8, 2 * groups), 0)
    target = 2 * ((here + wanted // 2 - 1 + groups) % groups) + wanted % 2
    row = lax.broadcasted_iota(jnp.int32, (8, 2 * groups), 1)
    rows = jnp.dot((row == target).astype(BF16), near[...], preferred_element_type=F32)
    own_id = group[:, 2:3].astype(F32)
    total = tally = 0.0
    for beside in range(3):
        ids = rows[2 * beside : 2 * beside + 1, 0:count]
        ratio = rows[2 * beside : 2 * beside + 1, count : 2 * count]
        ratio = ratio + rows[2 * beside + 1 : 2 * beside + 2, 0:count]
        ratio = ratio + rows[2 * beside + 1 : 2 * beside + 2, count : 2 * count]
        same = (own_id == ids).astype(F32)
        tally = tally + jnp.sum(same, axis=1, keepdims=True)
        total = total + jnp.sum(same * ratio, axis=1, keepdims=True)
    sequence = lax.broadcasted_iota(jnp.int32, (count, advantage.shape[1]), 1).astype(F32)
    own = jnp.sum(jnp.where(own_id == sequence, advantage[...], 0.0), axis=1, keepdims=True)
    weight = own * jnp.minimum(jnp.exp(total / tally), CLIP_HIGH)
    out[...] = jnp.broadcast_to(weight, out.shape)


def cut_of(offset, width):
    return pl.multiple_of((lax.axis_index("tp") + offset + CUTS) % CUTS * width, width)


def forward_kernel(x0, xm1, xp1, x2, w_gate, w_up, w_down, y0, ym1, yp1, y2, gate_out, up_out):
    width = x0.shape[1]
    gate_pre = up_pre = 0.0
    for rows, offset in ((x0, 0), (xm1, -1), (xp1, 1), (x2, 2)):
        cut = pl.ds(cut_of(offset, width), width)
        gate_pre += jnp.dot(rows[...], w_gate[cut, :], preferred_element_type=F32)
        up_pre += jnp.dot(rows[...], w_up[cut, :], preferred_element_type=F32)
    gate_out[...] = gate_pre
    up_out[...] = up_pre
    hidden = (gate_pre * jax.nn.sigmoid(gate_pre) * up_pre).astype(BF16)
    for rows, offset in ((y2, 2), (yp1, 1), (ym1, -1), (y0, 0)):
        cut = pl.ds(cut_of(offset, width), width)
        rows[...] = jnp.dot(hidden, w_down[:, cut], preferred_element_type=F32).astype(BF16)


def backward_kernel(d0, dm1, dp1, d2, gate, up, w_gate, w_up, w_down, g0, gm1, gp1, g2):
    width = d0.shape[1]
    contract = (((1,), (1,)), ((), ()))
    d_hidden = 0.0
    for rows, offset in ((d0, 0), (dm1, -1), (dp1, 1), (d2, 2)):
        cut = pl.ds(cut_of(offset, width), width)
        d_hidden += lax.dot_general(
            rows[...], w_down[:, cut], contract, preferred_element_type=F32
        )
    gate_pre = gate[...]
    squash = jax.nn.sigmoid(gate_pre)
    d_gate = (d_hidden * up[...] * squash * (1.0 + gate_pre * (1.0 - squash))).astype(BF16)
    d_up = (d_hidden * (gate_pre * squash)).astype(BF16)
    for rows, offset in ((g2, 2), (gp1, 1), (gm1, -1), (g0, 0)):
        cut = pl.ds(cut_of(offset, width), width)
        rows[...] = (
            lax.dot_general(d_gate, w_gate[cut, :], contract, preferred_element_type=F32)
            + lax.dot_general(d_up, w_up[cut, :], contract, preferred_element_type=F32)
        ).astype(BF16)


def sum_kernel(y0, y_right, y_left, g0, g_right, g_left, out):
    width = y0.shape[1]
    out[:, 0:width] = (
        y0[...].astype(F32) + y_right[...].astype(F32) + y_left[...].astype(F32)
    ).astype(BF16)
    out[:, width : 2 * width] = (
        g0[...].astype(F32) + g_right[...].astype(F32) + g_left[...].astype(F32)
    ).astype(BF16)


def combine_kernel(back, group, weights, out):
    slots, both = back.shape
    width = both // 2
    count = group.shape[0]
    meta = group[:, both : both + META].astype(F32)
    hots = slot_one_hots(meta, slots // 2, 2)
    weight = weights[:, 0:1]
    upstream = group[:, width:both].astype(F32)
    total = 0.0
    columns = []
    for k in range(2):
        picked = jnp.dot(hots[k].astype(BF16), back[...], preferred_element_type=F32)
        first = 6 + 3 * k
        gate = meta[:, first : first + 1] + meta[:, first + 1 : first + 2]
        gate = gate + meta[:, first + 2 : first + 3]
        total = total + gate * picked
        term = weight * jnp.sum(upstream * picked[:, 0:width], axis=1, keepdims=True)
        columns += list(split3(term))
    out[:, 0:width] = total[:, 0:width].astype(BF16)
    out[:, width:both] = (weight * total[:, width:both]).astype(BF16)
    out[:, both : both + META] = lanes(count, columns).astype(BF16)


def unpack_kernel(arrived, mixed, grad_tokens, grad_gates):
    parts, rows = arrived.shape[0], arrived.shape[1]
    width = mixed.shape[1] // CUTS
    terms = jnp.zeros((rows, META), F32)
    for t in range(parts):
        terms += arrived[t, :, 2 * width : 2 * width + META].astype(F32)
    for q in range(CUTS):
        total = 0.0
        for t in range(q, parts, CUTS):
            total = total + arrived[t, :, 0 : 2 * width].astype(F32)
        cut = slice(q * width, (q + 1) * width)
        mixed[:, cut] = total[:, 0:width].astype(BF16)
        grad_tokens[:, cut] = total[:, width : 2 * width].astype(BF16)
    for k in range(2):
        column = (
            terms[:, 3 * k : 3 * k + 1]
            + terms[:, 3 * k + 1 : 3 * k + 2]
            + terms[:, 3 * k + 2 : 3 * k + 3]
        )
        grad_gates[k : k + 1, :] = row_of(column, rows)


def call(kernel, shapes, *operands, mib=8):
    return pl.pallas_call(
        kernel,
        out_shape=shapes,
        compiler_params=pltpu.CompilerParams(vmem_limit_bytes=mib * 1024 * 1024),
    )(*operands)


def struct(*shape, dtype=BF16):
    return jax.ShapeDtypeStruct(shape, dtype)


def shift(rows, places):
    size = lax.axis_size("tp")
    return lax.ppermute(rows, "tp", [(i, (i + places) % size) for i in range(size)])


def add(left, right):
    return (left.astype(F32) + right.astype(F32)).astype(BF16)


def per_device(
    tokens, routes, gate_weights, seq_ids, log_ratio, advantage, upstream, w_gate, w_up, w_down
):
    count, model = tokens.shape
    parts = lax.axis_size("tp")
    groups = lax.axis_size("dp") * lax.axis_size("ctx")
    group_tokens = count * parts
    width = model // CUTS
    both = 2 * width
    slots = 2 * groups
    gate_local, up_local, down_local = w_gate[0], w_up[0], w_down[0]

    packed = call(
        pack_kernel,
        struct(parts, count, both + META),
        tokens,
        upstream,
        routes.T,
        gate_weights.T,
        seq_ids.reshape(1, count),
        log_ratio.reshape(1, count),
    )
    group = lax.all_to_all(packed, "tp", 0, 0).reshape(group_tokens, both + META)
    sent = call(dispatch_kernel, struct(slots, both + META), group)
    arrived = lax.all_to_all(
        sent.reshape(groups, 2, both + META), GROUP_AXES, 0, 0
    ).reshape(slots, both + META)

    x0, d0 = arrived[:, 0:width], arrived[:, width:both]
    xm1, dp1 = shift(x0, 1), shift(d0, -1)
    xp1, dm1 = shift(x0, -1), shift(d0, 1)
    x2, d2 = shift(xm1, 1), shift(dp1, -1)

    weights = call(
        weight_kernel,
        struct(group_tokens, META, dtype=F32),
        arrived[:, both:],
        group[:, both:],
        advantage.reshape(1, -1),
    )
    piece = struct(slots, width)
    inner = struct(slots, gate_local.shape[1], dtype=F32)
    y0, ym1, yp1, y2, gate_pre, up_pre = call(
        forward_kernel,
        (piece,) * 4 + (inner,) * 2,
        x0, xm1, xp1, x2, gate_local, up_local, down_local,
        mib=16,
    )
    g0, gm1, gp1, g2 = call(
        backward_kernel,
        (piece,) * 4,
        d0, dm1, dp1, d2, gate_pre, up_pre, gate_local, up_local, down_local,
        mib=16,
    )
    y_right = shift(yp1, 1)
    y_left = shift(add(ym1, shift(y2, -1)), -1)
    g_left = shift(gm1, -1)
    g_right = shift(add(gp1, shift(g2, 1)), 1)
    summed = call(sum_kernel, struct(slots, both), y0, y_right, y_left, g0, g_right, g_left)

    back = lax.all_to_all(summed.reshape(groups, 2, both), GROUP_AXES, 0, 0)
    combined = call(
        combine_kernel,
        struct(group_tokens, both + META),
        back.reshape(slots, both),
        group,
        weights,
    )
    home = lax.all_to_all(combined.reshape(parts, count, both + META), "tp", 0, 0)
    mixed, grad_tokens, grad_gates = call(
        unpack_kernel,
        (struct(count, model), struct(count, model), struct(2, count, dtype=F32)),
        home,
    )
    return mixed, grad_tokens, grad_gates.T


def solution(mesh):
    rows = ("dp", "ctx", "tp")
    in_specs = (
        P(rows, None),
        P(rows, None),
        P(rows, None),
        P(rows),
        P(rows),
        P(),
        P(rows, None),
        P(GROUP_AXES, None, "tp"),
        P(GROUP_AXES, None, "tp"),
        P(GROUP_AXES, "tp", None),
    )
    out_specs = (P(rows, None), P(rows, None), P(rows, None))
    return jax.shard_map(
        per_device, mesh=mesh, in_specs=in_specs, out_specs=out_specs, check_vma=False
    )
```

```python
import jax
import jax.numpy as jnp
from jax import lax
from jax.experimental import pallas as pl
from jax.experimental.pallas import tpu as pltpu
from jax.sharding import PartitionSpec as P

CLIP_HIGH = 1.2
GROUP_AXES = ("dp", "ctx")
META = 128
CUTS = 4
F32 = jnp.float32
BF16 = jnp.bfloat16


def split3(value):
    high = value.astype(BF16).astype(F32)
    rest = value - high
    middle = rest.astype(BF16).astype(F32)
    return high, middle, rest - middle


def columns_of(rows_by_one, count):
    eye = lax.broadcasted_iota(jnp.int32, (count, count), 0) == lax.broadcasted_iota(
        jnp.int32, (count, count), 1
    )
    return jnp.sum(jnp.where(eye, rows_by_one, 0.0), axis=1, keepdims=True)


def row_of(column, count):
    eye = lax.broadcasted_iota(jnp.int32, (count, count), 0) == lax.broadcasted_iota(
        jnp.int32, (count, count), 1
    )
    return jnp.sum(jnp.where(eye, column, 0.0), axis=0, keepdims=True)


def lanes(rows, columns):
    lane = lax.broadcasted_iota(jnp.int32, (rows, META), 1)
    total = jnp.zeros((rows, META), F32)
    for place, column in enumerate(columns):
        total = total + jnp.where(lane == place, column, 0.0)
    return total


def pack_kernel(tokens, upstream, routes, gates, ids, ratio, out):
    parts, rows = out.shape[0], out.shape[1]
    width = tokens.shape[1] // CUTS
    rows_in = [routes[0:1, :].astype(F32), routes[1:2, :].astype(F32), ids[...].astype(F32)]
    rows_in += list(split3(ratio[...]))
    gate_parts = split3(gates[...])
    for k in range(2):
        rows_in += [piece[k : k + 1, :] for piece in gate_parts]
    meta = lanes(rows, [columns_of(row, rows) for row in rows_in]).astype(BF16)
    for t in range(parts):
        cut = slice((t % CUTS) * width, (t % CUTS + 1) * width)
        out[t, :, 0:width] = tokens[:, cut]
        out[t, :, width : 2 * width] = upstream[:, cut]
        out[t, :, 2 * width : 2 * width + META] = meta


def slot_one_hots(meta, experts, capacity):
    count = meta.shape[0]
    expert = lax.broadcasted_iota(jnp.int32, (count, experts), 1).astype(F32)
    chosen = [(meta[:, k : k + 1] == expert).astype(F32) for k in range(2)]
    row = lax.broadcasted_iota(jnp.int32, (count, count), 0)
    column = lax.broadcasted_iota(jnp.int32, (count, count), 1)
    before = jnp.dot(
        (column < row).astype(BF16),
        (chosen[0] + chosen[1]).astype(BF16),
        preferred_element_type=F32,
    )
    slot = lax.broadcasted_iota(jnp.int32, (count, experts * capacity), 1).astype(F32)
    result = []
    for k in range(2):
        position = jnp.sum(before * chosen[k], axis=1, keepdims=True)
        result.append((meta[:, k : k + 1] * capacity + position == slot).astype(F32))
    return result


def dispatch_kernel(group, out):
    slots = out.shape[0]
    width = out.shape[1] - META
    meta = group[:, width : width + META].astype(F32)
    hots = slot_one_hots(meta, slots // 2, 2)
    out[:, 0:width] = lax.dot_general(
        (hots[0] + hots[1]).astype(BF16),
        group[:, 0:width],
        (((0,), (0,)), ((), ())),
        preferred_element_type=F32,
    ).astype(BF16)
    across = meta.T
    first = jnp.concatenate([across[2:3, :], across[3:4, :]], axis=1)
    second = jnp.concatenate([across[4:5, :], across[5:6, :]], axis=1)
    odd = lax.broadcasted_iota(jnp.int32, (slots, META), 0) % 2 == 1
    out[:, width : width + META] = jnp.where(odd, second, first).astype(BF16)


def arrive_kernel(arrived, x, dy, near):
    rows = arrived.shape[0] * arrived.shape[1]
    width = x.shape[1]
    x[...] = arrived[:, :, 0:width].reshape(rows, width)
    dy[...] = arrived[:, :, width : 2 * width].reshape(rows, width)
    near[...] = arrived[:, :, 2 * width :].reshape(rows, META)


def weight_kernel(near, group, advantage, out):
    groups = near.shape[0] // 2
    count = group.shape[0]
    here = lax.axis_index("dp") * lax.axis_size("ctx") + lax.axis_index("ctx")
    wanted = lax.broadcasted_iota(jnp.int32, (8, 2 * groups), 0)
    target = 2 * ((here + wanted // 2 - 1 + groups) % groups) + wanted % 2
    row = lax.broadcasted_iota(jnp.int32, (8, 2 * groups), 1)
    rows = jnp.dot((row == target).astype(BF16), near[...], preferred_element_type=F32)
    own_id = group[:, 2:3].astype(F32)
    total = tally = 0.0
    for beside in range(3):
        ids = rows[2 * beside : 2 * beside + 1, 0:count]
        ratio = rows[2 * beside : 2 * beside + 1, count : 2 * count]
        ratio = ratio + rows[2 * beside + 1 : 2 * beside + 2, 0:count]
        ratio = ratio + rows[2 * beside + 1 : 2 * beside + 2, count : 2 * count]
        same = (own_id == ids).astype(F32)
        tally = tally + jnp.sum(same, axis=1, keepdims=True)
        total = total + jnp.sum(same * ratio, axis=1, keepdims=True)
    sequence = lax.broadcasted_iota(jnp.int32, (count, advantage.shape[1]), 1).astype(F32)
    own = jnp.sum(jnp.where(own_id == sequence, advantage[...], 0.0), axis=1, keepdims=True)
    weight = own * jnp.minimum(jnp.exp(total / tally), CLIP_HIGH)
    out[...] = jnp.broadcast_to(weight, out.shape)


def cut_of(offset, width):
    return pl.multiple_of((lax.axis_index("tp") + offset + CUTS) % CUTS * width, width)


def forward_kernel(x0, xm1, xp1, x2, w_gate, w_up, w_down, y0, ym1, yp1, y2, gate_out, up_out):
    width = x0.shape[1]
    gate_pre = up_pre = 0.0
    for rows, offset in ((x0, 0), (xm1, -1), (xp1, 1), (x2, 2)):
        cut = pl.ds(cut_of(offset, width), width)
        gate_pre += jnp.dot(rows[...], w_gate[cut, :], preferred_element_type=F32)
        up_pre += jnp.dot(rows[...], w_up[cut, :], preferred_element_type=F32)
    gate_out[...] = gate_pre
    up_out[...] = up_pre
    hidden = (gate_pre * jax.nn.sigmoid(gate_pre) * up_pre).astype(BF16)
    for rows, offset in ((y2, 2), (yp1, 1), (ym1, -1), (y0, 0)):
        cut = pl.ds(cut_of(offset, width), width)
        rows[...] = jnp.dot(hidden, w_down[:, cut], preferred_element_type=F32).astype(BF16)


def backward_kernel(d0, dm1, dp1, d2, gate, up, w_gate, w_up, w_down, g0, gm1, gp1, g2):
    width = d0.shape[1]
    contract = (((1,), (1,)), ((), ()))
    d_hidden = 0.0
    for rows, offset in ((d0, 0), (dm1, -1), (dp1, 1), (d2, 2)):
        cut = pl.ds(cut_of(offset, width), width)
        d_hidden += lax.dot_general(
            rows[...], w_down[:, cut], contract, preferred_element_type=F32
        )
    gate_pre = gate[...]
    squash = jax.nn.sigmoid(gate_pre)
    d_gate = (d_hidden * up[...] * squash * (1.0 + gate_pre * (1.0 - squash))).astype(BF16)
    d_up = (d_hidden * (gate_pre * squash)).astype(BF16)
    for rows, offset in ((g2, 2), (gp1, 1), (gm1, -1), (g0, 0)):
        cut = pl.ds(cut_of(offset, width), width)
        rows[...] = (
            lax.dot_general(d_gate, w_gate[cut, :], contract, preferred_element_type=F32)
            + lax.dot_general(d_up, w_up[cut, :], contract, preferred_element_type=F32)
        ).astype(BF16)


def sum_kernel(y0, y_right, y_left, g0, g_right, g_left, out):
    width = y0.shape[1]
    shape = (out.shape[0], out.shape[1], width)
    out[:, :, 0:width] = (
        (y0[...].astype(F32) + y_right[...].astype(F32) + y_left[...].astype(F32))
        .astype(BF16)
        .reshape(shape)
    )
    out[:, :, width : 2 * width] = (
        (g0[...].astype(F32) + g_right[...].astype(F32) + g_left[...].astype(F32))
        .astype(BF16)
        .reshape(shape)
    )


def combine_kernel(back, group, weights, out):
    slots, both = back.shape
    width = both // 2
    count = group.shape[0]
    meta = group[:, both : both + META].astype(F32)
    hots = slot_one_hots(meta, slots // 2, 2)
    weight = weights[:, 0:1]
    upstream = group[:, width:both].astype(F32)
    total = 0.0
    columns = []
    for k in range(2):
        picked = jnp.dot(hots[k].astype(BF16), back[...], preferred_element_type=F32)
        first = 6 + 3 * k
        gate = meta[:, first : first + 1] + meta[:, first + 1 : first + 2]
        gate = gate + meta[:, first + 2 : first + 3]
        total = total + gate * picked
        term = weight * jnp.sum(upstream * picked[:, 0:width], axis=1, keepdims=True)
        columns += list(split3(term))
    out[:, 0:width] = total[:, 0:width].astype(BF16)
    out[:, width:both] = (weight * total[:, width:both]).astype(BF16)
    out[:, both : both + META] = lanes(count, columns).astype(BF16)


def unpack_kernel(arrived, mixed, grad_tokens, grad_gates):
    parts, rows = arrived.shape[0], arrived.shape[1]
    width = mixed.shape[1] // CUTS
    terms = jnp.zeros((rows, META), F32)
    for t in range(parts):
        terms += arrived[t, :, 2 * width : 2 * width + META].astype(F32)
    for q in range(CUTS):
        total = 0.0
        for t in range(q, parts, CUTS):
            total = total + arrived[t, :, 0 : 2 * width].astype(F32)
        cut = slice(q * width, (q + 1) * width)
        mixed[:, cut] = total[:, 0:width].astype(BF16)
        grad_tokens[:, cut] = total[:, width : 2 * width].astype(BF16)
    for k in range(2):
        column = (
            terms[:, 3 * k : 3 * k + 1]
            + terms[:, 3 * k + 1 : 3 * k + 2]
            + terms[:, 3 * k + 2 : 3 * k + 3]
        )
        grad_gates[k : k + 1, :] = row_of(column, rows)


def call(kernel, shapes, *operands, mib=8, flops=0):
    return pl.pallas_call(
        kernel,
        out_shape=shapes,
        cost_estimate=pl.CostEstimate(flops=flops, bytes_accessed=0, transcendentals=0),
        compiler_params=pltpu.CompilerParams(vmem_limit_bytes=mib * 1024 * 1024),
    )(*operands)


def struct(*shape, dtype=BF16):
    return jax.ShapeDtypeStruct(shape, dtype)


def shift(rows, places):
    size = lax.axis_size("tp")
    return lax.ppermute(rows, "tp", [(i, (i + places) % size) for i in range(size)])


def add(left, right):
    return (left.astype(F32) + right.astype(F32)).astype(BF16)


def per_device(
    tokens, routes, gate_weights, seq_ids, log_ratio, advantage, upstream, w_gate, w_up, w_down
):
    count, model = tokens.shape
    parts = lax.axis_size("tp")
    groups = lax.axis_size("dp") * lax.axis_size("ctx")
    group_tokens = count * parts
    width = model // CUTS
    both = 2 * width
    slots = 2 * groups
    gate_local, up_local, down_local = w_gate[0], w_up[0], w_down[0]

    packed = call(
        pack_kernel,
        struct(parts, count, both + META),
        tokens,
        upstream,
        routes.T,
        gate_weights.T,
        seq_ids.reshape(1, count),
        log_ratio.reshape(1, count),
    )
    group = lax.all_to_all(packed, "tp", 0, 0).reshape(group_tokens, both + META)
    sent = call(dispatch_kernel, struct(slots, both + META), group)
    arrived = lax.all_to_all(sent.reshape(groups, 2, both + META), GROUP_AXES, 0, 0)
    x0, d0, near = call(
        arrive_kernel, (struct(slots, width), struct(slots, width), struct(slots, META)), arrived
    )
    xm1, dp1 = shift(x0, 1), shift(d0, -1)
    xp1, dm1 = shift(x0, -1), shift(d0, 1)
    x2, d2 = shift(xm1, 1), shift(dp1, -1)

    weights = call(
        weight_kernel,
        struct(group_tokens, META, dtype=F32),
        near,
        group[:, both:],
        advantage.reshape(1, -1),
    )
    piece = struct(slots, width)
    inner = struct(slots, gate_local.shape[1], dtype=F32)
    y0, ym1, yp1, y2, gate_pre, up_pre = call(
        forward_kernel,
        (piece,) * 4 + (inner,) * 2,
        x0, xm1, xp1, x2, gate_local, up_local, down_local,
        mib=16,
    )
    g0, gm1, gp1, g2 = call(
        backward_kernel,
        (piece,) * 4,
        d0, dm1, dp1, d2, gate_pre, up_pre, gate_local, up_local, down_local,
        mib=16,
    )
    y_right = shift(yp1, 1)
    y_left = shift(add(ym1, shift(y2, -1)), -1)
    g_left = shift(gm1, -1)
    g_right = shift(add(gp1, shift(g2, 1)), 1)
    summed = call(sum_kernel, struct(groups, 2, both), y0, y_right, y_left, g0, g_right, g_left)

    back = lax.all_to_all(summed, GROUP_AXES, 0, 0)
    combined = call(
        combine_kernel,
        struct(group_tokens, both + META),
        back.reshape(slots, both),
        group,
        weights,
    )
    home = lax.all_to_all(combined.reshape(parts, count, both + META), "tp", 0, 0)
    mixed, grad_tokens, grad_gates = call(
        unpack_kernel,
        (struct(count, model), struct(count, model), struct(2, count, dtype=F32)),
        home,
    )
    return mixed, grad_tokens, grad_gates.T


def solution(mesh):
    rows = ("dp", "ctx", "tp")
    in_specs = (
        P(rows, None),
        P(rows, None),
        P(rows, None),
        P(rows),
        P(rows),
        P(),
        P(rows, None),
        P(GROUP_AXES, None, "tp"),
        P(GROUP_AXES, None, "tp"),
        P(GROUP_AXES, "tp", None),
    )
    out_specs = (P(rows, None), P(rows, None), P(rows, None))
    return jax.shard_map(
        per_device, mesh=mesh, in_specs=in_specs, out_specs=out_specs, check_vma=False
    )
```

```python
import jax
import jax.numpy as jnp
from jax import lax
from jax.experimental import pallas as pl
from jax.experimental.pallas import tpu as pltpu
from jax.sharding import PartitionSpec as P

CLIP_HIGH = 1.2
GROUP_AXES = ("dp", "ctx")
META = 128
CUTS = 4
PACK_MIB = 60
F32 = jnp.float32
BF16 = jnp.bfloat16


def split3(value):
    high = value.astype(BF16).astype(F32)
    rest = value - high
    middle = rest.astype(BF16).astype(F32)
    return high, middle, rest - middle


def columns_of(rows_by_one, count):
    eye = lax.broadcasted_iota(jnp.int32, (count, count), 0) == lax.broadcasted_iota(
        jnp.int32, (count, count), 1
    )
    return jnp.sum(jnp.where(eye, rows_by_one, 0.0), axis=1, keepdims=True)


def row_of(column, count):
    eye = lax.broadcasted_iota(jnp.int32, (count, count), 0) == lax.broadcasted_iota(
        jnp.int32, (count, count), 1
    )
    return jnp.sum(jnp.where(eye, column, 0.0), axis=0, keepdims=True)


def lanes(rows, columns):
    lane = lax.broadcasted_iota(jnp.int32, (rows, META), 1)
    total = jnp.zeros((rows, META), F32)
    for place, column in enumerate(columns):
        total = total + jnp.where(lane == place, column, 0.0)
    return total


def pack_kernel(
    tokens_in, upstream_in, routes_in, gates_in, ids_in, ratio_in, advantage_in,
    out, tokens, upstream, routes, gates, ids, ratio, advantage, sems,
):
    pairs = (
        (tokens_in, tokens), (upstream_in, upstream), (routes_in, routes),
        (gates_in, gates), (ids_in, ids), (ratio_in, ratio), (advantage_in, advantage),
    )
    copies = [
        pltpu.make_async_copy(source, target, sems.at[place])
        for place, (source, target) in enumerate(pairs)
    ]
    for copy in copies:
        copy.start()
    for copy in copies[::-1]:
        copy.wait()
    parts, rows = out.shape[0], out.shape[1]
    width = tokens.shape[1] // CUTS
    rows_in = [routes[0:1, :].astype(F32), routes[1:2, :].astype(F32), ids[...].astype(F32)]
    rows_in += list(split3(ratio[...]))
    gate_parts = split3(gates[...])
    for k in range(2):
        rows_in += [piece[k : k + 1, :] for piece in gate_parts]
    columns = [columns_of(row, rows) for row in rows_in]
    sequence = lax.broadcasted_iota(jnp.int32, (rows, advantage.shape[1]), 1).astype(F32)
    own = jnp.where(columns[2] == sequence, advantage[...], 0.0)
    columns += list(split3(jnp.sum(own, axis=1, keepdims=True)))
    meta = lanes(rows, columns).astype(BF16)
    for t in range(parts):
        cut = slice((t % CUTS) * width, (t % CUTS + 1) * width)
        out[t, :, 0:width] = tokens[:, cut]
        out[t, :, width : 2 * width] = upstream[:, cut]
        out[t, :, 2 * width : 2 * width + META] = meta


def slot_one_hots(meta, experts, capacity):
    count = meta.shape[0]
    expert = lax.broadcasted_iota(jnp.int32, (count, experts), 1).astype(F32)
    chosen = [(meta[:, k : k + 1] == expert).astype(F32) for k in range(2)]
    row = lax.broadcasted_iota(jnp.int32, (count, count), 0)
    column = lax.broadcasted_iota(jnp.int32, (count, count), 1)
    before = jnp.dot(
        (column < row).astype(BF16),
        (chosen[0] + chosen[1]).astype(BF16),
        preferred_element_type=F32,
    )
    slot = lax.broadcasted_iota(jnp.int32, (count, experts * capacity), 1).astype(F32)
    result = []
    for k in range(2):
        position = jnp.sum(before * chosen[k], axis=1, keepdims=True)
        result.append((meta[:, k : k + 1] * capacity + position == slot).astype(F32))
    return result


def dispatch_kernel(group, out, hot_out):
    slots = out.shape[0]
    width = out.shape[1] - META
    meta = group[:, width : width + META].astype(F32)
    hots = slot_one_hots(meta, slots // 2, 2)
    for k in range(2):
        hot_out[k] = hots[k].astype(BF16)
    out[:, 0:width] = lax.dot_general(
        (hots[0] + hots[1]).astype(BF16),
        group[:, 0:width],
        (((0,), (0,)), ((), ())),
        preferred_element_type=F32,
    ).astype(BF16)
    across = meta.T
    first = jnp.concatenate([across[2:3, :], across[3:4, :]], axis=1)
    second = jnp.concatenate([across[4:5, :], across[5:6, :]], axis=1)
    odd = lax.broadcasted_iota(jnp.int32, (slots, META), 0) % 2 == 1
    out[:, width : width + META] = jnp.where(odd, second, first).astype(BF16)


def arrive_kernel(arrived, x, dy, near):
    rows = arrived.shape[0] * arrived.shape[1]
    width = x.shape[1]
    x[...] = arrived[:, :, 0:width].reshape(rows, width)
    dy[...] = arrived[:, :, width : 2 * width].reshape(rows, width)
    near[...] = arrived[:, :, 2 * width :].reshape(rows, META)


def sequence_weights(near, meta):
    groups = near.shape[0] // 2
    count = meta.shape[0]
    here = lax.axis_index("dp") * lax.axis_size("ctx") + lax.axis_index("ctx")
    wanted = lax.broadcasted_iota(jnp.int32, (8, 2 * groups), 0)
    target = 2 * ((here + wanted // 2 - 1 + groups) % groups) + wanted % 2
    row = lax.broadcasted_iota(jnp.int32, (8, 2 * groups), 1)
    rows = jnp.dot((row == target).astype(BF16), near[...], preferred_element_type=F32)
    own_id = meta[:, 2:3].astype(F32)
    total = tally = 0.0
    for beside in range(3):
        ids = rows[2 * beside : 2 * beside + 1, 0:count]
        ratio = rows[2 * beside : 2 * beside + 1, count : 2 * count]
        ratio = ratio + rows[2 * beside + 1 : 2 * beside + 2, 0:count]
        ratio = ratio + rows[2 * beside + 1 : 2 * beside + 2, count : 2 * count]
        same = (own_id == ids).astype(F32)
        tally = tally + jnp.sum(same, axis=1, keepdims=True)
        total = total + jnp.sum(same * ratio, axis=1, keepdims=True)
    own = meta[:, 12:13].astype(F32) + meta[:, 13:14].astype(F32) + meta[:, 14:15].astype(F32)
    return own * jnp.minimum(jnp.exp(total / tally), CLIP_HIGH)


def cut_of(offset, width):
    return pl.multiple_of((lax.axis_index("tp") + offset + CUTS) % CUTS * width, width)


def forward_kernel(
    x0, xm1, xp1, x2, near, group, w_gate, w_up, w_down,
    y0, ym1, yp1, y2, gate_out, up_out, weights,
):
    width = x0.shape[1]
    weight = sequence_weights(near, group[:, group.shape[1] - META :])
    weights[...] = jnp.broadcast_to(weight, weights.shape)
    gate_pre = up_pre = 0.0
    for rows, offset in ((x0, 0), (xm1, -1), (xp1, 1), (x2, 2)):
        cut = pl.ds(cut_of(offset, width), width)
        gate_pre += jnp.dot(rows[...], w_gate[cut, :], preferred_element_type=F32)
        up_pre += jnp.dot(rows[...], w_up[cut, :], preferred_element_type=F32)
    gate_out[...] = gate_pre
    up_out[...] = up_pre
    hidden = (gate_pre * jax.nn.sigmoid(gate_pre) * up_pre).astype(BF16)
    for rows, offset in ((y2, 2), (yp1, 1), (ym1, -1), (y0, 0)):
        cut = pl.ds(cut_of(offset, width), width)
        rows[...] = jnp.dot(hidden, w_down[:, cut], preferred_element_type=F32).astype(BF16)


def backward_kernel(d0, dm1, dp1, d2, gate, up, w_gate, w_up, w_down, g0, gm1, gp1, g2):
    width = d0.shape[1]
    contract = (((1,), (1,)), ((), ()))
    d_hidden = 0.0
    for rows, offset in ((d0, 0), (dm1, -1), (dp1, 1), (d2, 2)):
        cut = pl.ds(cut_of(offset, width), width)
        d_hidden += lax.dot_general(
            rows[...], w_down[:, cut], contract, preferred_element_type=F32
        )
    gate_pre = gate[...]
    squash = jax.nn.sigmoid(gate_pre)
    d_gate = (d_hidden * up[...] * squash * (1.0 + gate_pre * (1.0 - squash))).astype(BF16)
    d_up = (d_hidden * (gate_pre * squash)).astype(BF16)
    for rows, offset in ((g2, 2), (gp1, 1), (gm1, -1), (g0, 0)):
        cut = pl.ds(cut_of(offset, width), width)
        rows[...] = (
            lax.dot_general(d_gate, w_gate[cut, :], contract, preferred_element_type=F32)
            + lax.dot_general(d_up, w_up[cut, :], contract, preferred_element_type=F32)
        ).astype(BF16)


def sum_kernel(y0, g0, left, y_right, g_right, out):
    slots, width = y0.shape
    shape = (out.shape[0], out.shape[1], width)
    for own, right, half in ((y0, y_right, 0), (g0, g_right, 1)):
        total = own[...].astype(F32) + right[...].astype(F32)
        total = total + left[half * slots : (half + 1) * slots, :].astype(F32)
        out[:, :, half * width : (half + 1) * width] = total.astype(BF16).reshape(shape)


def combine_kernel(back, group, weights, hots, out):
    slots, both = back.shape[0] * back.shape[1], back.shape[2]
    width = both // 2
    count = group.shape[0]
    returned = back[...].reshape(slots, both)
    meta = group[:, both : both + META].astype(F32)
    weight = weights[:, 0:1]
    upstream = group[:, width:both].astype(F32)
    total = 0.0
    columns = []
    for k in range(2):
        picked = jnp.dot(hots[k], returned, preferred_element_type=F32)
        first = 6 + 3 * k
        gate = meta[:, first : first + 1] + meta[:, first + 1 : first + 2]
        gate = gate + meta[:, first + 2 : first + 3]
        total = total + gate * picked
        term = weight * jnp.sum(upstream * picked[:, 0:width], axis=1, keepdims=True)
        columns += list(split3(term))
    out[:, 0:width] = total[:, 0:width].astype(BF16)
    out[:, width:both] = (weight * total[:, width:both]).astype(BF16)
    out[:, both : both + META] = lanes(count, columns).astype(BF16)


def unpack_kernel(arrived, mixed, grad_tokens, grad_gates):
    parts, rows = arrived.shape[0], arrived.shape[1]
    width = mixed.shape[1] // CUTS
    terms = jnp.zeros((rows, META), F32)
    for t in range(parts):
        terms += arrived[t, :, 2 * width : 2 * width + META].astype(F32)
    for q in range(CUTS):
        total = 0.0
        for t in range(q, parts, CUTS):
            total = total + arrived[t, :, 0 : 2 * width].astype(F32)
        cut = slice(q * width, (q + 1) * width)
        mixed[:, cut] = total[:, 0:width].astype(BF16)
        grad_tokens[:, cut] = total[:, width : 2 * width].astype(BF16)
    for k in range(2):
        column = (
            terms[:, 3 * k : 3 * k + 1]
            + terms[:, 3 * k + 1 : 3 * k + 2]
            + terms[:, 3 * k + 2 : 3 * k + 3]
        )
        grad_gates[k : k + 1, :] = row_of(column, rows)


def call(kernel, shapes, *operands, mib=8, flops=0):
    return pl.pallas_call(
        kernel,
        out_shape=shapes,
        cost_estimate=pl.CostEstimate(flops=flops, bytes_accessed=0, transcendentals=0),
        compiler_params=pltpu.CompilerParams(vmem_limit_bytes=mib * 1024 * 1024),
    )(*operands)


def struct(*shape, dtype=BF16):
    return jax.ShapeDtypeStruct(shape, dtype)


def shift(rows, places):
    size = lax.axis_size("tp")
    return lax.ppermute(rows, "tp", [(i, (i + places) % size) for i in range(size)])


def add(left, right):
    return (left.astype(F32) + right.astype(F32)).astype(BF16)


def per_device(
    tokens, routes, gate_weights, seq_ids, log_ratio, advantage, upstream, w_gate, w_up, w_down
):
    count, model = tokens.shape
    parts = lax.axis_size("tp")
    groups = lax.axis_size("dp") * lax.axis_size("ctx")
    group_tokens = count * parts
    width = model // CUTS
    both = 2 * width
    slots = 2 * groups
    gate_local, up_local, down_local = w_gate[0], w_up[0], w_down[0]

    local = (
        tokens,
        upstream,
        routes.T,
        gate_weights.T,
        seq_ids.reshape(1, count),
        log_ratio.reshape(1, count),
        advantage.reshape(1, -1),
    )
    packed = pl.pallas_call(
        pack_kernel,
        out_shape=struct(parts, count, both + META),
        in_specs=[pl.BlockSpec(memory_space=pltpu.HBM)] * len(local),
        scratch_shapes=[pltpu.VMEM(array.shape, array.dtype) for array in local]
        + [pltpu.SemaphoreType.DMA((len(local),))],
        compiler_params=pltpu.CompilerParams(vmem_limit_bytes=PACK_MIB * 1024 * 1024),
    )(*local)
    group = lax.all_to_all(packed, "tp", 0, 0).reshape(group_tokens, both + META)
    sent, hots = call(
        dispatch_kernel, (struct(slots, both + META), struct(2, group_tokens, slots)), group
    )
    arrived = lax.all_to_all(sent.reshape(groups, 2, both + META), GROUP_AXES, 0, 0)
    x0, d0, near = call(
        arrive_kernel, (struct(slots, width), struct(slots, width), struct(slots, META)), arrived
    )
    xm1, dp1 = shift(x0, 1), shift(d0, -1)
    xp1, dm1 = shift(x0, -1), shift(d0, 1)
    x2, d2 = shift(xm1, 1), shift(dp1, -1)

    piece = struct(slots, width)
    inner = struct(slots, gate_local.shape[1], dtype=F32)
    y0, ym1, yp1, y2, gate_pre, up_pre, weights = call(
        forward_kernel,
        (piece,) * 4 + (inner,) * 2 + (struct(group_tokens, META, dtype=F32),),
        x0, xm1, xp1, x2, near, group, gate_local, up_local, down_local,
        mib=16,
    )
    g0, gm1, gp1, g2 = call(
        backward_kernel,
        (piece,) * 4,
        d0, dm1, dp1, d2, gate_pre, up_pre, gate_local, up_local, down_local,
        mib=16,
    )
    y_far, y_right, g_far = shift(y2, -1), shift(yp1, 1), shift(g2, 1)
    left = shift(jnp.concatenate([add(ym1, y_far), gm1], axis=0), -1)
    g_right = shift(add(gp1, g_far), 1)
    summed = call(sum_kernel, struct(groups, 2, both), y0, g0, left, y_right, g_right)

    back = lax.all_to_all(summed, GROUP_AXES, 0, 0)
    combined = call(
        combine_kernel,
        struct(group_tokens, both + META),
        back,
        group,
        weights,
        hots,
    )
    home = lax.all_to_all(combined.reshape(parts, count, both + META), "tp", 0, 0)
    mixed, grad_tokens, grad_gates = call(
        unpack_kernel,
        (struct(count, model), struct(count, model), struct(2, count, dtype=F32)),
        home,
    )
    return mixed, grad_tokens, grad_gates.T


def solution(mesh):
    rows = ("dp", "ctx", "tp")
    in_specs = (
        P(rows, None),
        P(rows, None),
        P(rows, None),
        P(rows),
        P(rows),
        P(),
        P(rows, None),
        P(GROUP_AXES, None, "tp"),
        P(GROUP_AXES, None, "tp"),
        P(GROUP_AXES, "tp", None),
    )
    out_specs = (P(rows, None), P(rows, None), P(rows, None))
    return jax.shard_map(
        per_device, mesh=mesh, in_specs=in_specs, out_specs=out_specs, check_vma=False
    )
```

```python
import jax
import jax.numpy as jnp
from jax import lax
from jax.experimental import pallas as pl
from jax.experimental.pallas import tpu as pltpu
from jax.sharding import PartitionSpec as P

CLIP_HIGH = 1.2
GROUP_AXES = ("dp", "ctx")
META = 128
CUTS = 4
PACK_MIB = 60
F32 = jnp.float32
BF16 = jnp.bfloat16


def split3(value):
    high = value.astype(BF16).astype(F32)
    rest = value - high
    middle = rest.astype(BF16).astype(F32)
    return high, middle, rest - middle


def columns_of(rows_by_one, count):
    eye = lax.broadcasted_iota(jnp.int32, (count, count), 0) == lax.broadcasted_iota(
        jnp.int32, (count, count), 1
    )
    return jnp.sum(jnp.where(eye, rows_by_one, 0.0), axis=1, keepdims=True)


def row_of(column, count):
    eye = lax.broadcasted_iota(jnp.int32, (count, count), 0) == lax.broadcasted_iota(
        jnp.int32, (count, count), 1
    )
    return jnp.sum(jnp.where(eye, column, 0.0), axis=0, keepdims=True)


def lanes(rows, columns):
    lane = lax.broadcasted_iota(jnp.int32, (rows, META), 1)
    total = jnp.zeros((rows, META), F32)
    for place, column in enumerate(columns):
        total = total + jnp.where(lane == place, column, 0.0)
    return total


def pack_kernel(tokens, upstream, routes, gates, ids, ratio, advantage, out):
    parts, rows = out.shape[0], out.shape[1]
    width = tokens.shape[1] // CUTS
    rows_in = [routes[0:1, :].astype(F32), routes[1:2, :].astype(F32), ids[...].astype(F32)]
    rows_in += list(split3(ratio[...]))
    gate_parts = split3(gates[...])
    for k in range(2):
        rows_in += [piece[k : k + 1, :] for piece in gate_parts]
    columns = [columns_of(row, rows) for row in rows_in]
    sequence = lax.broadcasted_iota(jnp.int32, (rows, advantage.shape[1]), 1).astype(F32)
    own = jnp.where(columns[2] == sequence, advantage[...], 0.0)
    columns += list(split3(jnp.sum(own, axis=1, keepdims=True)))
    meta = lanes(rows, columns).astype(BF16)
    for t in range(parts):
        cut = slice((t % CUTS) * width, (t % CUTS + 1) * width)
        out[t, :, 0:width] = tokens[:, cut]
        out[t, :, width : 2 * width] = upstream[:, cut]
        out[t, :, 2 * width : 2 * width + META] = meta


def slot_one_hots(meta, experts, capacity):
    count = meta.shape[0]
    expert = lax.broadcasted_iota(jnp.int32, (count, experts), 1).astype(F32)
    chosen = [(meta[:, k : k + 1] == expert).astype(F32) for k in range(2)]
    row = lax.broadcasted_iota(jnp.int32, (count, count), 0)
    column = lax.broadcasted_iota(jnp.int32, (count, count), 1)
    before = jnp.dot(
        (column < row).astype(BF16),
        (chosen[0] + chosen[1]).astype(BF16),
        preferred_element_type=F32,
    )
    slot = lax.broadcasted_iota(jnp.int32, (count, experts * capacity), 1).astype(F32)
    result = []
    for k in range(2):
        position = jnp.sum(before * chosen[k], axis=1, keepdims=True)
        result.append((meta[:, k : k + 1] * capacity + position == slot).astype(F32))
    return result


def dispatch_kernel(group, out, hot_out):
    slots = out.shape[0]
    width = out.shape[1] - META
    meta = group[:, width : width + META].astype(F32)
    hots = slot_one_hots(meta, slots // 2, 2)
    for k in range(2):
        hot_out[k] = hots[k].astype(BF16)
    out[:, 0:width] = lax.dot_general(
        (hots[0] + hots[1]).astype(BF16),
        group[:, 0:width],
        (((0,), (0,)), ((), ())),
        preferred_element_type=F32,
    ).astype(BF16)
    across = meta.T
    first = jnp.concatenate([across[2:3, :], across[3:4, :]], axis=1)
    second = jnp.concatenate([across[4:5, :], across[5:6, :]], axis=1)
    odd = lax.broadcasted_iota(jnp.int32, (slots, META), 0) % 2 == 1
    out[:, width : width + META] = jnp.where(odd, second, first).astype(BF16)


def arrive_kernel(arrived, x, dy, near):
    rows = arrived.shape[0] * arrived.shape[1]
    width = x.shape[1]
    x[...] = arrived[:, :, 0:width].reshape(rows, width)
    dy[...] = arrived[:, :, width : 2 * width].reshape(rows, width)
    near[...] = arrived[:, :, 2 * width :].reshape(rows, META)


def sequence_weights(near, meta):
    groups = near.shape[0] // 2
    count = meta.shape[0]
    here = lax.axis_index("dp") * lax.axis_size("ctx") + lax.axis_index("ctx")
    wanted = lax.broadcasted_iota(jnp.int32, (8, 2 * groups), 0)
    target = 2 * ((here + wanted // 2 - 1 + groups) % groups) + wanted % 2
    row = lax.broadcasted_iota(jnp.int32, (8, 2 * groups), 1)
    rows = jnp.dot((row == target).astype(BF16), near[...], preferred_element_type=F32)
    own_id = meta[:, 2:3].astype(F32)
    total = tally = 0.0
    for beside in range(3):
        ids = rows[2 * beside : 2 * beside + 1, 0:count]
        ratio = rows[2 * beside : 2 * beside + 1, count : 2 * count]
        ratio = ratio + rows[2 * beside + 1 : 2 * beside + 2, 0:count]
        ratio = ratio + rows[2 * beside + 1 : 2 * beside + 2, count : 2 * count]
        same = (own_id == ids).astype(F32)
        tally = tally + jnp.sum(same, axis=1, keepdims=True)
        total = total + jnp.sum(same * ratio, axis=1, keepdims=True)
    own = meta[:, 12:13].astype(F32) + meta[:, 13:14].astype(F32) + meta[:, 14:15].astype(F32)
    return own * jnp.minimum(jnp.exp(total / tally), CLIP_HIGH)


def cut_of(offset, width):
    return pl.multiple_of((lax.axis_index("tp") + offset + CUTS) % CUTS * width, width)


def forward_kernel(
    x0, xm1, xp1, x2, near, group, w_gate, w_up, w_down,
    y0, ym1, yp1, y2, gate_out, up_out, weights,
):
    width = x0.shape[1]
    weight = sequence_weights(near, group[:, group.shape[1] - META :])
    weights[...] = jnp.broadcast_to(weight, weights.shape)
    gate_pre = up_pre = 0.0
    for rows, offset in ((x0, 0), (xm1, -1), (xp1, 1), (x2, 2)):
        cut = pl.ds(cut_of(offset, width), width)
        gate_pre += jnp.dot(rows[...], w_gate[cut, :], preferred_element_type=F32)
        up_pre += jnp.dot(rows[...], w_up[cut, :], preferred_element_type=F32)
    gate_out[...] = gate_pre
    up_out[...] = up_pre
    hidden = (gate_pre * jax.nn.sigmoid(gate_pre) * up_pre).astype(BF16)
    for rows, offset in ((y2, 2), (yp1, 1), (ym1, -1), (y0, 0)):
        cut = pl.ds(cut_of(offset, width), width)
        rows[...] = jnp.dot(hidden, w_down[:, cut], preferred_element_type=F32).astype(BF16)


CONTRACT_LAST = (((1,), (1,)), ((), ()))


def input_grad(d_gate, d_up, w_gate, w_up, cut):
    total = lax.dot_general(d_gate, w_gate[cut, :], CONTRACT_LAST, preferred_element_type=F32)
    total += lax.dot_general(d_up, w_up[cut, :], CONTRACT_LAST, preferred_element_type=F32)
    return total.astype(BF16)


def backward_kernel(d0, dm1, dp1, d2, gate, up, w_gate, w_up, w_down, g2, gate_out, up_out):
    width = d0.shape[1]
    d_hidden = 0.0
    for rows, offset in ((d0, 0), (dm1, -1), (dp1, 1), (d2, 2)):
        cut = pl.ds(cut_of(offset, width), width)
        d_hidden += lax.dot_general(
            rows[...], w_down[:, cut], CONTRACT_LAST, preferred_element_type=F32
        )
    gate_pre = gate[...]
    squash = jax.nn.sigmoid(gate_pre)
    d_gate = (d_hidden * up[...] * squash * (1.0 + gate_pre * (1.0 - squash))).astype(BF16)
    d_up = (d_hidden * (gate_pre * squash)).astype(BF16)
    gate_out[...] = d_gate
    up_out[...] = d_up
    g2[...] = input_grad(d_gate, d_up, w_gate, w_up, pl.ds(cut_of(2, width), width))


def rest_kernel(d_gate, d_up, w_gate, w_up, g0, gm1, gp1):
    width = g0.shape[1]
    for rows, offset in ((gm1, -1), (gp1, 1), (g0, 0)):
        cut = pl.ds(cut_of(offset, width), width)
        rows[...] = input_grad(d_gate[...], d_up[...], w_gate, w_up, cut)


def sum_kernel(y0, g0, left, y_right, g_right, out):
    slots, width = y0.shape
    shape = (out.shape[0], out.shape[1], width)
    for own, right, half in ((y0, y_right, 0), (g0, g_right, 1)):
        total = own[...].astype(F32) + right[...].astype(F32)
        total = total + left[half * slots : (half + 1) * slots, :].astype(F32)
        out[:, :, half * width : (half + 1) * width] = total.astype(BF16).reshape(shape)


def combine_kernel(back, group, weights, hots, out):
    slots, both = back.shape[0] * back.shape[1], back.shape[2]
    width = both // 2
    count = group.shape[0]
    returned = back[...].reshape(slots, both)
    meta = group[:, both : both + META].astype(F32)
    weight = weights[:, 0:1]
    upstream = group[:, width:both].astype(F32)
    total = 0.0
    columns = []
    for k in range(2):
        picked = jnp.dot(hots[k], returned, preferred_element_type=F32)
        first = 6 + 3 * k
        gate = meta[:, first : first + 1] + meta[:, first + 1 : first + 2]
        gate = gate + meta[:, first + 2 : first + 3]
        total = total + gate * picked
        term = weight * jnp.sum(upstream * picked[:, 0:width], axis=1, keepdims=True)
        columns += list(split3(term))
    out[:, 0:width] = total[:, 0:width].astype(BF16)
    out[:, width:both] = (weight * total[:, width:both]).astype(BF16)
    out[:, both : both + META] = lanes(count, columns).astype(BF16)


def unpack_kernel(arrived, mixed, grad_tokens, grad_gates):
    parts, rows = arrived.shape[0], arrived.shape[1]
    width = mixed.shape[1] // CUTS
    terms = jnp.zeros((rows, META), F32)
    for t in range(parts):
        terms += arrived[t, :, 2 * width : 2 * width + META].astype(F32)
    for q in range(CUTS):
        total = 0.0
        for t in range(q, parts, CUTS):
            total = total + arrived[t, :, 0 : 2 * width].astype(F32)
        cut = slice(q * width, (q + 1) * width)
        mixed[:, cut] = total[:, 0:width].astype(BF16)
        grad_tokens[:, cut] = total[:, width : 2 * width].astype(BF16)
    for k in range(2):
        column = (
            terms[:, 3 * k : 3 * k + 1]
            + terms[:, 3 * k + 1 : 3 * k + 2]
            + terms[:, 3 * k + 2 : 3 * k + 3]
        )
        grad_gates[k : k + 1, :] = row_of(column, rows)


def call(kernel, shapes, *operands, mib=8):
    return pl.pallas_call(
        kernel,
        out_shape=shapes,
        cost_estimate=pl.CostEstimate(flops=0, bytes_accessed=0, transcendentals=0),
        compiler_params=pltpu.CompilerParams(vmem_limit_bytes=mib * 1024 * 1024),
    )(*operands)


def struct(*shape, dtype=BF16):
    return jax.ShapeDtypeStruct(shape, dtype)


def shift(rows, places):
    size = lax.axis_size("tp")
    return lax.ppermute(rows, "tp", [(i, (i + places) % size) for i in range(size)])


def add(left, right):
    return (left.astype(F32) + right.astype(F32)).astype(BF16)


def per_device(
    tokens, routes, gate_weights, seq_ids, log_ratio, advantage, upstream, w_gate, w_up, w_down
):
    count, model = tokens.shape
    parts = lax.axis_size("tp")
    groups = lax.axis_size("dp") * lax.axis_size("ctx")
    group_tokens = count * parts
    width = model // CUTS
    both = 2 * width
    slots = 2 * groups
    gate_local, up_local, down_local = w_gate[0], w_up[0], w_down[0]

    packed = call(
        pack_kernel,
        struct(parts, count, both + META),
        tokens,
        upstream,
        routes.T,
        gate_weights.T,
        seq_ids.reshape(1, count),
        log_ratio.reshape(1, count),
        advantage.reshape(1, -1),
        mib=PACK_MIB,
    )
    group = lax.all_to_all(packed, "tp", 0, 0).reshape(group_tokens, both + META)
    sent, hots = call(
        dispatch_kernel, (struct(slots, both + META), struct(2, group_tokens, slots)), group
    )
    arrived = lax.all_to_all(sent.reshape(groups, 2, both + META), GROUP_AXES, 0, 0)
    x0, d0, near = call(
        arrive_kernel, (struct(slots, width), struct(slots, width), struct(slots, META)), arrived
    )
    xm1, dp1 = shift(x0, 1), shift(d0, -1)
    xp1, dm1 = shift(x0, -1), shift(d0, 1)
    x2, d2 = shift(xm1, 1), shift(dp1, -1)

    piece = struct(slots, width)
    inner = struct(slots, gate_local.shape[1], dtype=F32)
    y0, ym1, yp1, y2, gate_pre, up_pre, weights = call(
        forward_kernel,
        (piece,) * 4 + (inner,) * 2 + (struct(group_tokens, META, dtype=F32),),
        x0, xm1, xp1, x2, near, group, gate_local, up_local, down_local,
        mib=16,
    )
    slope = struct(slots, gate_local.shape[1])
    g2, d_gate, d_up = call(
        backward_kernel,
        (piece, slope, slope),
        d0, dm1, dp1, d2, gate_pre, up_pre, gate_local, up_local, down_local,
        mib=16,
    )
    g0, gm1, gp1 = call(
        rest_kernel, (piece,) * 3, d_gate, d_up, gate_local, up_local, mib=16
    )
    y_far, y_right, g_far = shift(y2, -1), shift(yp1, 1), shift(g2, 1)
    left = shift(jnp.concatenate([add(ym1, y_far), gm1], axis=0), -1)
    g_right = shift(add(gp1, g_far), 1)
    summed = call(sum_kernel, struct(groups, 2, both), y0, g0, left, y_right, g_right)

    back = lax.all_to_all(summed, GROUP_AXES, 0, 0)
    combined = call(
        combine_kernel,
        struct(group_tokens, both + META),
        back,
        group,
        weights,
        hots,
    )
    home = lax.all_to_all(combined.reshape(parts, count, both + META), "tp", 0, 0)
    mixed, grad_tokens, grad_gates = call(
        unpack_kernel,
        (struct(count, model), struct(count, model), struct(2, count, dtype=F32)),
        home,
    )
    return mixed, grad_tokens, grad_gates.T


def solution(mesh):
    rows = ("dp", "ctx", "tp")
    in_specs = (
        P(rows, None),
        P(rows, None),
        P(rows, None),
        P(rows),
        P(rows),
        P(),
        P(rows, None),
        P(GROUP_AXES, None, "tp"),
        P(GROUP_AXES, None, "tp"),
        P(GROUP_AXES, "tp", None),
    )
    out_specs = (P(rows, None), P(rows, None), P(rows, None))
    return jax.shard_map(
        per_device, mesh=mesh, in_specs=in_specs, out_specs=out_specs, check_vma=False
    )
```

```python
import jax
import jax.numpy as jnp
from jax import lax
from jax.experimental import pallas as pl
from jax.experimental.pallas import tpu as pltpu
from jax.sharding import PartitionSpec as P

CLIP_HIGH = 1.2
GROUP_AXES = ("dp", "ctx")
META = 128
CUTS = 4
PACK_MIB = 60
F32 = jnp.float32
BF16 = jnp.bfloat16


def split3(value):
    high = value.astype(BF16).astype(F32)
    rest = value - high
    middle = rest.astype(BF16).astype(F32)
    return high, middle, rest - middle


def columns_of(rows_by_one, count):
    eye = lax.broadcasted_iota(jnp.int32, (count, count), 0) == lax.broadcasted_iota(
        jnp.int32, (count, count), 1
    )
    return jnp.sum(jnp.where(eye, rows_by_one, 0.0), axis=1, keepdims=True)


def row_of(column, count):
    eye = lax.broadcasted_iota(jnp.int32, (count, count), 0) == lax.broadcasted_iota(
        jnp.int32, (count, count), 1
    )
    return jnp.sum(jnp.where(eye, column, 0.0), axis=0, keepdims=True)


def lanes(rows, columns):
    lane = lax.broadcasted_iota(jnp.int32, (rows, META), 1)
    total = jnp.zeros((rows, META), F32)
    for place, column in enumerate(columns):
        total = total + jnp.where(lane == place, column, 0.0)
    return total


def pack_kernel(tokens, upstream, routes, gates, ids, ratio, advantage, out):
    parts, rows = out.shape[0], out.shape[1]
    width = tokens.shape[1] // CUTS
    rows_in = [routes[0:1, :].astype(F32), routes[1:2, :].astype(F32), ids[...].astype(F32)]
    rows_in += list(split3(ratio[...]))
    gate_parts = split3(gates[...])
    for k in range(2):
        rows_in += [piece[k : k + 1, :] for piece in gate_parts]
    columns = [columns_of(row, rows) for row in rows_in]
    sequence = lax.broadcasted_iota(jnp.int32, (rows, advantage.shape[1]), 1).astype(F32)
    own = jnp.where(columns[2] == sequence, advantage[...], 0.0)
    columns += list(split3(jnp.sum(own, axis=1, keepdims=True)))
    meta = lanes(rows, columns).astype(BF16)
    for t in range(parts):
        cut = slice((t % CUTS) * width, (t % CUTS + 1) * width)
        out[t, :, 0:width] = tokens[:, cut]
        out[t, :, width : 2 * width] = upstream[:, cut]
        out[t, :, 2 * width : 2 * width + META] = meta


def slot_one_hots(meta, experts, capacity):
    count = meta.shape[0]
    expert = lax.broadcasted_iota(jnp.int32, (count, experts), 1).astype(F32)
    chosen = [(meta[:, k : k + 1] == expert).astype(F32) for k in range(2)]
    row = lax.broadcasted_iota(jnp.int32, (count, count), 0)
    column = lax.broadcasted_iota(jnp.int32, (count, count), 1)
    before = jnp.dot(
        (column < row).astype(BF16),
        (chosen[0] + chosen[1]).astype(BF16),
        preferred_element_type=F32,
    )
    slot = lax.broadcasted_iota(jnp.int32, (count, experts * capacity), 1).astype(F32)
    result = []
    for k in range(2):
        position = jnp.sum(before * chosen[k], axis=1, keepdims=True)
        result.append((meta[:, k : k + 1] * capacity + position == slot).astype(F32))
    return result


def dispatch_kernel(group, out, hot_out):
    slots = out.shape[0] * out.shape[1]
    width = out.shape[2] - META
    meta = group[:, width : width + META].astype(F32)
    hots = slot_one_hots(meta, slots // 2, 2)
    for k in range(2):
        hot_out[k] = hots[k].astype(BF16)
    rows = lax.dot_general(
        (hots[0] + hots[1]).astype(BF16),
        group[:, 0:width],
        (((0,), (0,)), ((), ())),
        preferred_element_type=F32,
    ).astype(BF16)
    out[:, :, 0:width] = rows.reshape(out.shape[0], out.shape[1], width)
    across = meta.T
    first = jnp.concatenate([across[2:3, :], across[3:4, :]], axis=1)
    second = jnp.concatenate([across[4:5, :], across[5:6, :]], axis=1)
    odd = lax.broadcasted_iota(jnp.int32, (slots, META), 0) % 2 == 1
    beside = jnp.where(odd, second, first).astype(BF16)
    out[:, :, width : width + META] = beside.reshape(out.shape[0], out.shape[1], META)


def arrive_kernel(arrived, x, dy, near):
    rows = arrived.shape[0] * arrived.shape[1]
    width = x.shape[1]
    x[...] = arrived[:, :, 0:width].reshape(rows, width)
    dy[...] = arrived[:, :, width : 2 * width].reshape(rows, width)
    near[...] = arrived[:, :, 2 * width :].reshape(rows, META)


def sequence_weights(near, meta):
    groups = near.shape[0] // 2
    count = meta.shape[0]
    here = lax.axis_index("dp") * lax.axis_size("ctx") + lax.axis_index("ctx")
    wanted = lax.broadcasted_iota(jnp.int32, (8, 2 * groups), 0)
    target = 2 * ((here + wanted // 2 - 1 + groups) % groups) + wanted % 2
    row = lax.broadcasted_iota(jnp.int32, (8, 2 * groups), 1)
    rows = jnp.dot((row == target).astype(BF16), near[...], preferred_element_type=F32)
    own_id = meta[:, 2:3].astype(F32)
    total = tally = 0.0
    for beside in range(3):
        ids = rows[2 * beside : 2 * beside + 1, 0:count]
        ratio = rows[2 * beside : 2 * beside + 1, count : 2 * count]
        ratio = ratio + rows[2 * beside + 1 : 2 * beside + 2, 0:count]
        ratio = ratio + rows[2 * beside + 1 : 2 * beside + 2, count : 2 * count]
        same = (own_id == ids).astype(F32)
        tally = tally + jnp.sum(same, axis=1, keepdims=True)
        total = total + jnp.sum(same * ratio, axis=1, keepdims=True)
    own = meta[:, 12:13].astype(F32) + meta[:, 13:14].astype(F32) + meta[:, 14:15].astype(F32)
    return own * jnp.minimum(jnp.exp(total / tally), CLIP_HIGH)


def cut_of(offset, width):
    return pl.multiple_of((lax.axis_index("tp") + offset + CUTS) % CUTS * width, width)


def forward_kernel(
    x0, xm1, xp1, x2, near, group, w_gate, w_up, w_down,
    y0, ym1, yp1, y2, gate_out, up_out, weights,
):
    width = x0.shape[1]
    weight = sequence_weights(near, group[:, group.shape[1] - META :])
    weights[...] = jnp.broadcast_to(weight, weights.shape)
    gate_pre = up_pre = 0.0
    for rows, offset in ((x0, 0), (xm1, -1), (xp1, 1), (x2, 2)):
        cut = pl.ds(cut_of(offset, width), width)
        gate_pre += jnp.dot(rows[...], w_gate[cut, :], preferred_element_type=F32)
        up_pre += jnp.dot(rows[...], w_up[cut, :], preferred_element_type=F32)
    gate_out[...] = gate_pre
    up_out[...] = up_pre
    hidden = (gate_pre * jax.nn.sigmoid(gate_pre) * up_pre).astype(BF16)
    for rows, offset in ((y2, 2), (yp1, 1), (ym1, -1), (y0, 0)):
        cut = pl.ds(cut_of(offset, width), width)
        rows[...] = jnp.dot(hidden, w_down[:, cut], preferred_element_type=F32).astype(BF16)


CONTRACT_LAST = (((1,), (1,)), ((), ()))


def input_grad(d_gate, d_up, w_gate, w_up, cut):
    total = lax.dot_general(d_gate, w_gate[cut, :], CONTRACT_LAST, preferred_element_type=F32)
    total += lax.dot_general(d_up, w_up[cut, :], CONTRACT_LAST, preferred_element_type=F32)
    return total.astype(BF16)


def backward_kernel(d0, dm1, dp1, d2, gate, up, w_gate, w_up, w_down, g2, gate_out, up_out):
    width = d0.shape[1]
    d_hidden = 0.0
    for rows, offset in ((d0, 0), (dm1, -1), (dp1, 1), (d2, 2)):
        cut = pl.ds(cut_of(offset, width), width)
        d_hidden += lax.dot_general(
            rows[...], w_down[:, cut], CONTRACT_LAST, preferred_element_type=F32
        )
    gate_pre = gate[...]
    squash = jax.nn.sigmoid(gate_pre)
    d_gate = (d_hidden * up[...] * squash * (1.0 + gate_pre * (1.0 - squash))).astype(BF16)
    d_up = (d_hidden * (gate_pre * squash)).astype(BF16)
    gate_out[...] = d_gate
    up_out[...] = d_up
    g2[...] = input_grad(d_gate, d_up, w_gate, w_up, pl.ds(cut_of(2, width), width))


def rest_kernel(d_gate, d_up, w_gate, w_up, g0, gm1, gp1):
    width = g0.shape[1]
    for rows, offset in ((gm1, -1), (gp1, 1), (g0, 0)):
        cut = pl.ds(cut_of(offset, width), width)
        rows[...] = input_grad(d_gate[...], d_up[...], w_gate, w_up, cut)


def sum_kernel(y0, g0, left, y_right, g_right, out):
    slots, width = y0.shape
    shape = (out.shape[0], out.shape[1], width)
    for own, right, half in ((y0, y_right, 0), (g0, g_right, 1)):
        total = own[...].astype(F32) + right[...].astype(F32)
        total = total + left[half * slots : (half + 1) * slots, :].astype(F32)
        out[:, :, half * width : (half + 1) * width] = total.astype(BF16).reshape(shape)


def combine_kernel(back, group, weights, hots, out):
    slots, both = back.shape[0] * back.shape[1], back.shape[2]
    width = both // 2
    count = group.shape[0]
    returned = back[...].reshape(slots, both)
    meta = group[:, both : both + META].astype(F32)
    weight = weights[:, 0:1]
    upstream = group[:, width:both].astype(F32)
    total = 0.0
    columns = []
    for k in range(2):
        picked = jnp.dot(hots[k], returned, preferred_element_type=F32)
        first = 6 + 3 * k
        gate = meta[:, first : first + 1] + meta[:, first + 1 : first + 2]
        gate = gate + meta[:, first + 2 : first + 3]
        total = total + gate * picked
        term = weight * jnp.sum(upstream * picked[:, 0:width], axis=1, keepdims=True)
        columns += list(split3(term))
    out[:, 0:width] = total[:, 0:width].astype(BF16)
    out[:, width:both] = (weight * total[:, width:both]).astype(BF16)
    out[:, both : both + META] = lanes(count, columns).astype(BF16)


def unpack_kernel(arrived, mixed, grad_tokens, grad_gates):
    parts, rows = arrived.shape[0], arrived.shape[1]
    width = mixed.shape[1] // CUTS
    terms = jnp.zeros((rows, META), F32)
    for t in range(parts):
        terms += arrived[t, :, 2 * width : 2 * width + META].astype(F32)
    for q in range(CUTS):
        total = 0.0
        for t in range(q, parts, CUTS):
            total = total + arrived[t, :, 0 : 2 * width].astype(F32)
        cut = slice(q * width, (q + 1) * width)
        mixed[:, cut] = total[:, 0:width].astype(BF16)
        grad_tokens[:, cut] = total[:, width : 2 * width].astype(BF16)
    for k in range(2):
        column = (
            terms[:, 3 * k : 3 * k + 1]
            + terms[:, 3 * k + 1 : 3 * k + 2]
            + terms[:, 3 * k + 2 : 3 * k + 3]
        )
        grad_gates[k : k + 1, :] = row_of(column, rows)


def call(kernel, shapes, *operands, mib=8):
    return pl.pallas_call(
        kernel,
        out_shape=shapes,
        cost_estimate=pl.CostEstimate(flops=0, bytes_accessed=0, transcendentals=0),
        compiler_params=pltpu.CompilerParams(vmem_limit_bytes=mib * 1024 * 1024),
    )(*operands)


def struct(*shape, dtype=BF16):
    return jax.ShapeDtypeStruct(shape, dtype)


def shift(rows, places):
    size = lax.axis_size("tp")
    return lax.ppermute(rows, "tp", [(i, (i + places) % size) for i in range(size)])


def add(left, right):
    return (left.astype(F32) + right.astype(F32)).astype(BF16)


def per_device(
    tokens, routes, gate_weights, seq_ids, log_ratio, advantage, upstream, w_gate, w_up, w_down
):
    count, model = tokens.shape
    parts = lax.axis_size("tp")
    groups = lax.axis_size("dp") * lax.axis_size("ctx")
    group_tokens = count * parts
    width = model // CUTS
    both = 2 * width
    slots = 2 * groups
    gate_local, up_local, down_local = w_gate[0], w_up[0], w_down[0]

    packed = call(
        pack_kernel,
        struct(parts, count, both + META),
        tokens,
        upstream,
        routes.T,
        gate_weights.T,
        seq_ids.reshape(1, count),
        log_ratio.reshape(1, count),
        advantage.reshape(1, -1),
        mib=PACK_MIB,
    )
    group = lax.all_to_all(packed, "tp", 0, 0).reshape(group_tokens, both + META)
    sent, hots = call(
        dispatch_kernel,
        (struct(groups, 2, both + META), struct(2, group_tokens, slots)),
        group,
    )
    arrived = lax.all_to_all(sent, GROUP_AXES, 0, 0)
    x0, d0, near = call(
        arrive_kernel, (struct(slots, width), struct(slots, width), struct(slots, META)), arrived
    )
    xm1, dp1 = shift(x0, 1), shift(d0, -1)
    xp1, dm1 = shift(x0, -1), shift(d0, 1)
    x2, d2 = shift(xm1, 1), shift(dp1, -1)

    piece = struct(slots, width)
    inner = struct(slots, gate_local.shape[1], dtype=F32)
    y0, ym1, yp1, y2, gate_pre, up_pre, weights = call(
        forward_kernel,
        (piece,) * 4 + (inner,) * 2 + (struct(group_tokens, META, dtype=F32),),
        x0, xm1, xp1, x2, near, group, gate_local, up_local, down_local,
        mib=16,
    )
    slope = struct(slots, gate_local.shape[1])
    g2, d_gate, d_up = call(
        backward_kernel,
        (piece, slope, slope),
        d0, dm1, dp1, d2, gate_pre, up_pre, gate_local, up_local, down_local,
        mib=16,
    )
    g0, gm1, gp1 = call(
        rest_kernel, (piece,) * 3, d_gate, d_up, gate_local, up_local, mib=16
    )
    y_far, y_right, g_far = shift(y2, -1), shift(yp1, 1), shift(g2, 1)
    left = shift(jnp.concatenate([add(ym1, y_far), gm1], axis=0), -1)
    g_right = shift(add(gp1, g_far), 1)
    summed = call(sum_kernel, struct(groups, 2, both), y0, g0, left, y_right, g_right)

    back = lax.all_to_all(summed, GROUP_AXES, 0, 0)
    combined = call(
        combine_kernel,
        struct(group_tokens, both + META),
        back,
        group,
        weights,
        hots,
    )
    home = lax.all_to_all(combined.reshape(parts, count, both + META), "tp", 0, 0)
    mixed, grad_tokens, grad_gates = call(
        unpack_kernel,
        (struct(count, model), struct(count, model), struct(2, count, dtype=F32)),
        home,
    )
    return mixed, grad_tokens, grad_gates.T


def solution(mesh):
    rows = ("dp", "ctx", "tp")
    in_specs = (
        P(rows, None),
        P(rows, None),
        P(rows, None),
        P(rows),
        P(rows),
        P(),
        P(rows, None),
        P(GROUP_AXES, None, "tp"),
        P(GROUP_AXES, None, "tp"),
        P(GROUP_AXES, "tp", None),
    )
    out_specs = (P(rows, None), P(rows, None), P(rows, None))
    return jax.shard_map(
        per_device, mesh=mesh, in_specs=in_specs, out_specs=out_specs, check_vma=False
    )
```

```python
import jax
import jax.numpy as jnp
from jax import lax
from jax.experimental import pallas as pl
from jax.experimental.pallas import tpu as pltpu
from jax.sharding import PartitionSpec as P

CLIP_HIGH = 1.2
GROUP_AXES = ("dp", "ctx")
META = 128
CUTS = 4
PACK_MIB = 60
F32 = jnp.float32
BF16 = jnp.bfloat16


def split3(value):
    high = value.astype(BF16).astype(F32)
    rest = value - high
    middle = rest.astype(BF16).astype(F32)
    return high, middle, rest - middle


def columns_of(rows_by_one, count):
    eye = lax.broadcasted_iota(jnp.int32, (count, count), 0) == lax.broadcasted_iota(
        jnp.int32, (count, count), 1
    )
    return jnp.sum(jnp.where(eye, rows_by_one, 0.0), axis=1, keepdims=True)


def row_of(column, count):
    eye = lax.broadcasted_iota(jnp.int32, (count, count), 0) == lax.broadcasted_iota(
        jnp.int32, (count, count), 1
    )
    return jnp.sum(jnp.where(eye, column, 0.0), axis=0, keepdims=True)


def lanes(rows, columns):
    lane = lax.broadcasted_iota(jnp.int32, (rows, META), 1)
    total = jnp.zeros((rows, META), F32)
    for place, column in enumerate(columns):
        total = total + jnp.where(lane == place, column, 0.0)
    return total


def pack_kernel(tokens, upstream, routes, gates, ids, ratio, advantage, out):
    parts, rows = out.shape[0], out.shape[1]
    width = tokens.shape[1] // CUTS
    rows_in = [routes[0:1, :].astype(F32), routes[1:2, :].astype(F32), ids[...].astype(F32)]
    rows_in += list(split3(ratio[...]))
    gate_parts = split3(gates[...])
    for k in range(2):
        rows_in += [piece[k : k + 1, :] for piece in gate_parts]
    columns = [columns_of(row, rows) for row in rows_in]
    sequence = lax.broadcasted_iota(jnp.int32, (rows, advantage.shape[1]), 1).astype(F32)
    own = jnp.where(columns[2] == sequence, advantage[...], 0.0)
    columns += list(split3(jnp.sum(own, axis=1, keepdims=True)))
    meta = lanes(rows, columns).astype(BF16)
    for t in range(parts):
        cut = slice((t % CUTS) * width, (t % CUTS + 1) * width)
        out[t, :, 0:width] = tokens[:, cut]
        out[t, :, width : 2 * width] = upstream[:, cut]
        out[t, :, 2 * width : 2 * width + META] = meta


def slot_one_hots(meta, experts, capacity):
    count = meta.shape[0]
    expert = lax.broadcasted_iota(jnp.int32, (count, experts), 1).astype(F32)
    chosen = [(meta[:, k : k + 1] == expert).astype(F32) for k in range(2)]
    row = lax.broadcasted_iota(jnp.int32, (count, count), 0)
    column = lax.broadcasted_iota(jnp.int32, (count, count), 1)
    before = jnp.dot(
        (column < row).astype(BF16),
        (chosen[0] + chosen[1]).astype(BF16),
        preferred_element_type=F32,
    )
    slot = lax.broadcasted_iota(jnp.int32, (count, experts * capacity), 1).astype(F32)
    result = []
    for k in range(2):
        position = jnp.sum(before * chosen[k], axis=1, keepdims=True)
        result.append((meta[:, k : k + 1] * capacity + position == slot).astype(F32))
    return result


def dispatch_kernel(group, out, hot_out):
    slots = out.shape[0] * out.shape[1]
    width = out.shape[2] - META
    meta = group[:, width : width + META].astype(F32)
    hots = slot_one_hots(meta, slots // 2, 2)
    for k in range(2):
        hot_out[k] = hots[k].astype(BF16)
    rows = lax.dot_general(
        (hots[0] + hots[1]).astype(BF16),
        group[:, 0:width],
        (((0,), (0,)), ((), ())),
        preferred_element_type=F32,
    ).astype(BF16)
    out[:, :, 0:width] = rows.reshape(out.shape[0], out.shape[1], width)
    across = meta.T
    first = jnp.concatenate([across[2:3, :], across[3:4, :]], axis=1)
    second = jnp.concatenate([across[4:5, :], across[5:6, :]], axis=1)
    odd = lax.broadcasted_iota(jnp.int32, (slots, META), 0) % 2 == 1
    beside = jnp.where(odd, second, first).astype(BF16)
    out[:, :, width : width + META] = beside.reshape(out.shape[0], out.shape[1], META)


def arrive_kernel(arrived, x, dy, near):
    rows = arrived.shape[0] * arrived.shape[1]
    width = x.shape[1]
    x[...] = arrived[:, :, 0:width].reshape(rows, width)
    dy[...] = arrived[:, :, width : 2 * width].reshape(rows, width)
    near[...] = arrived[:, :, 2 * width :].reshape(rows, META)


def sequence_weights(near, meta):
    groups = near.shape[0] // 2
    count = meta.shape[0]
    here = lax.axis_index("dp") * lax.axis_size("ctx") + lax.axis_index("ctx")
    wanted = lax.broadcasted_iota(jnp.int32, (8, 2 * groups), 0)
    target = 2 * ((here + wanted // 2 - 1 + groups) % groups) + wanted % 2
    row = lax.broadcasted_iota(jnp.int32, (8, 2 * groups), 1)
    rows = jnp.dot((row == target).astype(BF16), near[...], preferred_element_type=F32)
    own_id = meta[:, 2:3].astype(F32)
    total = tally = 0.0
    for beside in range(3):
        ids = rows[2 * beside : 2 * beside + 1, 0:count]
        ratio = rows[2 * beside : 2 * beside + 1, count : 2 * count]
        ratio = ratio + rows[2 * beside + 1 : 2 * beside + 2, 0:count]
        ratio = ratio + rows[2 * beside + 1 : 2 * beside + 2, count : 2 * count]
        same = (own_id == ids).astype(F32)
        tally = tally + jnp.sum(same, axis=1, keepdims=True)
        total = total + jnp.sum(same * ratio, axis=1, keepdims=True)
    own = meta[:, 12:13].astype(F32) + meta[:, 13:14].astype(F32) + meta[:, 14:15].astype(F32)
    return own * jnp.minimum(jnp.exp(total / tally), CLIP_HIGH)


def cut_of(offset, width):
    return pl.multiple_of((lax.axis_index("tp") + offset + CUTS) % CUTS * width, width)


def forward_first_kernel(x0, xm1, xp1, near, group, w_gate, w_up, gate, up, weights):
    width = x0.shape[1]
    weight = sequence_weights(near, group[:, group.shape[1] - META :])
    weights[...] = jnp.broadcast_to(weight, weights.shape)
    gate_pre = up_pre = 0.0
    for rows, offset in ((x0, 0), (xm1, -1), (xp1, 1)):
        cut = pl.ds(cut_of(offset, width), width)
        gate_pre += jnp.dot(rows[...], w_gate[cut, :], preferred_element_type=F32)
        up_pre += jnp.dot(rows[...], w_up[cut, :], preferred_element_type=F32)
    gate[...] = gate_pre
    up[...] = up_pre


def forward_kernel(x2, gate, up, w_gate, w_up, w_down, y2, hidden_out, gate_out, up_out):
    width = x2.shape[1]
    cut = pl.ds(cut_of(2, width), width)
    gate_pre = gate[...] + jnp.dot(x2[...], w_gate[cut, :], preferred_element_type=F32)
    up_pre = up[...] + jnp.dot(x2[...], w_up[cut, :], preferred_element_type=F32)
    gate_out[...] = gate_pre
    up_out[...] = up_pre
    hidden = (gate_pre * jax.nn.sigmoid(gate_pre) * up_pre).astype(BF16)
    hidden_out[...] = hidden
    y2[...] = jnp.dot(hidden, w_down[:, cut], preferred_element_type=F32).astype(BF16)


def forward_rest_kernel(hidden, w_down, y0, ym1, yp1):
    width = y0.shape[1]
    for rows, offset in ((yp1, 1), (ym1, -1), (y0, 0)):
        cut = pl.ds(cut_of(offset, width), width)
        rows[...] = jnp.dot(hidden[...], w_down[:, cut], preferred_element_type=F32).astype(BF16)


def backward_first_kernel(d0, dm1, dp1, w_down, out):
    width = d0.shape[1]
    d_hidden = 0.0
    for rows, offset in ((d0, 0), (dm1, -1), (dp1, 1)):
        cut = pl.ds(cut_of(offset, width), width)
        d_hidden += lax.dot_general(
            rows[...], w_down[:, cut], CONTRACT_LAST, preferred_element_type=F32
        )
    out[...] = d_hidden


CONTRACT_LAST = (((1,), (1,)), ((), ()))


def input_grad(d_gate, d_up, w_gate, w_up, cut):
    total = lax.dot_general(d_gate, w_gate[cut, :], CONTRACT_LAST, preferred_element_type=F32)
    total += lax.dot_general(d_up, w_up[cut, :], CONTRACT_LAST, preferred_element_type=F32)
    return total.astype(BF16)


def backward_kernel(d2, first, gate, up, w_gate, w_up, w_down, g2, gate_out, up_out):
    width = d2.shape[1]
    cut = pl.ds(cut_of(2, width), width)
    d_hidden = first[...] + lax.dot_general(
        d2[...], w_down[:, cut], CONTRACT_LAST, preferred_element_type=F32
    )
    gate_pre = gate[...]
    squash = jax.nn.sigmoid(gate_pre)
    d_gate = (d_hidden * up[...] * squash * (1.0 + gate_pre * (1.0 - squash))).astype(BF16)
    d_up = (d_hidden * (gate_pre * squash)).astype(BF16)
    gate_out[...] = d_gate
    up_out[...] = d_up
    g2[...] = input_grad(d_gate, d_up, w_gate, w_up, cut)


def rest_kernel(d_gate, d_up, w_gate, w_up, g0, gm1, gp1):
    width = g0.shape[1]
    for rows, offset in ((gm1, -1), (gp1, 1), (g0, 0)):
        cut = pl.ds(cut_of(offset, width), width)
        rows[...] = input_grad(d_gate[...], d_up[...], w_gate, w_up, cut)


def sum_kernel(y0, g0, left, y_right, g_right, out):
    slots, width = y0.shape
    shape = (out.shape[0], out.shape[1], width)
    for own, right, half in ((y0, y_right, 0), (g0, g_right, 1)):
        total = own[...].astype(F32) + right[...].astype(F32)
        total = total + left[half * slots : (half + 1) * slots, :].astype(F32)
        out[:, :, half * width : (half + 1) * width] = total.astype(BF16).reshape(shape)


def combine_kernel(back, group, weights, hots, out):
    slots, both = back.shape[0] * back.shape[1], back.shape[2]
    width = both // 2
    count = group.shape[0]
    returned = back[...].reshape(slots, both)
    meta = group[:, both : both + META].astype(F32)
    weight = weights[:, 0:1]
    upstream = group[:, width:both].astype(F32)
    total = 0.0
    columns = []
    for k in range(2):
        picked = jnp.dot(hots[k], returned, preferred_element_type=F32)
        first = 6 + 3 * k
        gate = meta[:, first : first + 1] + meta[:, first + 1 : first + 2]
        gate = gate + meta[:, first + 2 : first + 3]
        total = total + gate * picked
        term = weight * jnp.sum(upstream * picked[:, 0:width], axis=1, keepdims=True)
        columns += list(split3(term))
    out[:, 0:width] = total[:, 0:width].astype(BF16)
    out[:, width:both] = (weight * total[:, width:both]).astype(BF16)
    out[:, both : both + META] = lanes(count, columns).astype(BF16)


def unpack_kernel(arrived, mixed, grad_tokens, grad_gates):
    parts, rows = arrived.shape[0], arrived.shape[1]
    width = mixed.shape[1] // CUTS
    terms = jnp.zeros((rows, META), F32)
    for t in range(parts):
        terms += arrived[t, :, 2 * width : 2 * width + META].astype(F32)
    for q in range(CUTS):
        total = 0.0
        for t in range(q, parts, CUTS):
            total = total + arrived[t, :, 0 : 2 * width].astype(F32)
        cut = slice(q * width, (q + 1) * width)
        mixed[:, cut] = total[:, 0:width].astype(BF16)
        grad_tokens[:, cut] = total[:, width : 2 * width].astype(BF16)
    for k in range(2):
        column = (
            terms[:, 3 * k : 3 * k + 1]
            + terms[:, 3 * k + 1 : 3 * k + 2]
            + terms[:, 3 * k + 2 : 3 * k + 3]
        )
        grad_gates[k : k + 1, :] = row_of(column, rows)


def call(kernel, shapes, *operands, mib=8):
    return pl.pallas_call(
        kernel,
        out_shape=shapes,
        cost_estimate=pl.CostEstimate(flops=0, bytes_accessed=0, transcendentals=0),
        compiler_params=pltpu.CompilerParams(vmem_limit_bytes=mib * 1024 * 1024),
    )(*operands)


def struct(*shape, dtype=BF16):
    return jax.ShapeDtypeStruct(shape, dtype)


def shift(rows, places):
    size = lax.axis_size("tp")
    return lax.ppermute(rows, "tp", [(i, (i + places) % size) for i in range(size)])


def add(left, right):
    return (left.astype(F32) + right.astype(F32)).astype(BF16)


def per_device(
    tokens, routes, gate_weights, seq_ids, log_ratio, advantage, upstream, w_gate, w_up, w_down
):
    count, model = tokens.shape
    parts = lax.axis_size("tp")
    groups = lax.axis_size("dp") * lax.axis_size("ctx")
    group_tokens = count * parts
    width = model // CUTS
    both = 2 * width
    slots = 2 * groups
    gate_local, up_local, down_local = w_gate[0], w_up[0], w_down[0]

    packed = call(
        pack_kernel,
        struct(parts, count, both + META),
        tokens,
        upstream,
        routes.T,
        gate_weights.T,
        seq_ids.reshape(1, count),
        log_ratio.reshape(1, count),
        advantage.reshape(1, -1),
        mib=PACK_MIB,
    )
    group = lax.all_to_all(packed, "tp", 0, 0).reshape(group_tokens, both + META)
    sent, hots = call(
        dispatch_kernel,
        (struct(groups, 2, both + META), struct(2, group_tokens, slots)),
        group,
    )
    arrived = lax.all_to_all(sent, GROUP_AXES, 0, 0)
    x0, d0, near = call(
        arrive_kernel, (struct(slots, width), struct(slots, width), struct(slots, META)), arrived
    )
    xm1, dp1 = shift(x0, 1), shift(d0, -1)
    xp1, dm1 = shift(x0, -1), shift(d0, 1)
    x2, d2 = shift(xm1, 1), shift(dp1, -1)

    piece = struct(slots, width)
    inner = struct(slots, gate_local.shape[1], dtype=F32)
    gate_first, up_first, weights = call(
        forward_first_kernel,
        (inner, inner, struct(group_tokens, META, dtype=F32)),
        x0, xm1, xp1, near, group, gate_local, up_local,
        mib=16,
    )
    slope = struct(slots, gate_local.shape[1])
    y2, hidden, gate_pre, up_pre = call(
        forward_kernel,
        (piece, slope, inner, inner),
        x2, gate_first, up_first, gate_local, up_local, down_local,
        mib=16,
    )
    y0, ym1, yp1 = call(forward_rest_kernel, (piece,) * 3, hidden, down_local, mib=16)
    d_first = call(backward_first_kernel, inner, d0, dm1, dp1, down_local, mib=16)
    g2, d_gate, d_up = call(
        backward_kernel,
        (piece, slope, slope),
        d2, d_first, gate_pre, up_pre, gate_local, up_local, down_local,
        mib=16,
    )
    g0, gm1, gp1 = call(
        rest_kernel, (piece,) * 3, d_gate, d_up, gate_local, up_local, mib=16
    )
    y_far, y_right, g_far = shift(y2, -1), shift(yp1, 1), shift(g2, 1)
    left = shift(jnp.concatenate([add(ym1, y_far), gm1], axis=0), -1)
    g_right = shift(add(gp1, g_far), 1)
    summed = call(sum_kernel, struct(groups, 2, both), y0, g0, left, y_right, g_right)

    back = lax.all_to_all(summed, GROUP_AXES, 0, 0)
    combined = call(
        combine_kernel,
        struct(group_tokens, both + META),
        back,
        group,
        weights,
        hots,
    )
    home = lax.all_to_all(combined.reshape(parts, count, both + META), "tp", 0, 0)
    mixed, grad_tokens, grad_gates = call(
        unpack_kernel,
        (struct(count, model), struct(count, model), struct(2, count, dtype=F32)),
        home,
    )
    return mixed, grad_tokens, grad_gates.T


def solution(mesh):
    rows = ("dp", "ctx", "tp")
    in_specs = (
        P(rows, None),
        P(rows, None),
        P(rows, None),
        P(rows),
        P(rows),
        P(),
        P(rows, None),
        P(GROUP_AXES, None, "tp"),
        P(GROUP_AXES, None, "tp"),
        P(GROUP_AXES, "tp", None),
    )
    out_specs = (P(rows, None), P(rows, None), P(rows, None))
    return jax.shard_map(
        per_device, mesh=mesh, in_specs=in_specs, out_specs=out_specs, check_vma=False
    )
```

```python
import jax
import jax.numpy as jnp
from jax import lax
from jax.experimental import pallas as pl
from jax.experimental.pallas import tpu as pltpu
from jax.sharding import PartitionSpec as P

CLIP_HIGH = 1.2
GROUP_AXES = ("dp", "ctx")
META = 128
CUTS = 4
PACK_MIB = 60
F32 = jnp.float32
BF16 = jnp.bfloat16


def split3(value):
    high = value.astype(BF16).astype(F32)
    rest = value - high
    middle = rest.astype(BF16).astype(F32)
    return high, middle, rest - middle


def columns_of(rows_by_one, count):
    eye = lax.broadcasted_iota(jnp.int32, (count, count), 0) == lax.broadcasted_iota(
        jnp.int32, (count, count), 1
    )
    return jnp.sum(jnp.where(eye, rows_by_one, 0.0), axis=1, keepdims=True)


def row_of(column, count):
    eye = lax.broadcasted_iota(jnp.int32, (count, count), 0) == lax.broadcasted_iota(
        jnp.int32, (count, count), 1
    )
    return jnp.sum(jnp.where(eye, column, 0.0), axis=0, keepdims=True)


def lanes(rows, columns):
    lane = lax.broadcasted_iota(jnp.int32, (rows, META), 1)
    total = jnp.zeros((rows, META), F32)
    for place, column in enumerate(columns):
        total = total + jnp.where(lane == place, column, 0.0)
    return total


def pack_kernel(tokens, upstream, routes, gates, ids, ratio, advantage, out):
    parts, rows = out.shape[0], out.shape[1]
    width = tokens.shape[1] // CUTS
    rows_in = [routes[0:1, :].astype(F32), routes[1:2, :].astype(F32), ids[...].astype(F32)]
    rows_in += list(split3(ratio[...]))
    gate_parts = split3(gates[...])
    for k in range(2):
        rows_in += [piece[k : k + 1, :] for piece in gate_parts]
    columns = [columns_of(row, rows) for row in rows_in]
    sequence = lax.broadcasted_iota(jnp.int32, (rows, advantage.shape[1]), 1).astype(F32)
    own = jnp.where(columns[2] == sequence, advantage[...], 0.0)
    columns += list(split3(jnp.sum(own, axis=1, keepdims=True)))
    meta = lanes(rows, columns).astype(BF16)
    for t in range(parts):
        cut = slice((t % CUTS) * width, (t % CUTS + 1) * width)
        out[t, :, 0:width] = tokens[:, cut]
        out[t, :, width : 2 * width] = upstream[:, cut]
        out[t, :, 2 * width : 2 * width + META] = meta


def slot_one_hots(meta, experts, capacity):
    count = meta.shape[0]
    expert = lax.broadcasted_iota(jnp.int32, (count, experts), 1).astype(F32)
    chosen = [(meta[:, k : k + 1] == expert).astype(F32) for k in range(2)]
    row = lax.broadcasted_iota(jnp.int32, (count, count), 0)
    column = lax.broadcasted_iota(jnp.int32, (count, count), 1)
    before = jnp.dot(
        (column < row).astype(BF16),
        (chosen[0] + chosen[1]).astype(BF16),
        preferred_element_type=F32,
    )
    slot = lax.broadcasted_iota(jnp.int32, (count, experts * capacity), 1).astype(F32)
    result = []
    for k in range(2):
        position = jnp.sum(before * chosen[k], axis=1, keepdims=True)
        result.append((meta[:, k : k + 1] * capacity + position == slot).astype(F32))
    return result


def dispatch_kernel(group, out, hot_out):
    slots = out.shape[0] * out.shape[1]
    width = out.shape[2] - META
    meta = group[:, width : width + META].astype(F32)
    hots = slot_one_hots(meta, slots // 2, 2)
    for k in range(2):
        hot_out[k] = hots[k].astype(BF16)
    rows = lax.dot_general(
        (hots[0] + hots[1]).astype(BF16),
        group[:, 0:width],
        (((0,), (0,)), ((), ())),
        preferred_element_type=F32,
    ).astype(BF16)
    out[:, :, 0:width] = rows.reshape(out.shape[0], out.shape[1], width)
    across = meta.T
    first = jnp.concatenate([across[2:3, :], across[3:4, :]], axis=1)
    second = jnp.concatenate([across[4:5, :], across[5:6, :]], axis=1)
    odd = lax.broadcasted_iota(jnp.int32, (slots, META), 0) % 2 == 1
    beside = jnp.where(odd, second, first).astype(BF16)
    out[:, :, width : width + META] = beside.reshape(out.shape[0], out.shape[1], META)


def arrive_kernel(arrived, x, dy, near):
    rows = arrived.shape[0] * arrived.shape[1]
    width = x.shape[1]
    x[...] = arrived[:, :, 0:width].reshape(rows, width)
    dy[...] = arrived[:, :, width : 2 * width].reshape(rows, width)
    near[...] = arrived[:, :, 2 * width :].reshape(rows, META)


def sequence_weights(near, meta):
    groups = near.shape[0] // 2
    count = meta.shape[0]
    here = lax.axis_index("dp") * lax.axis_size("ctx") + lax.axis_index("ctx")
    wanted = lax.broadcasted_iota(jnp.int32, (8, 2 * groups), 0)
    target = 2 * ((here + wanted // 2 - 1 + groups) % groups) + wanted % 2
    row = lax.broadcasted_iota(jnp.int32, (8, 2 * groups), 1)
    rows = jnp.dot((row == target).astype(BF16), near[...], preferred_element_type=F32)
    own_id = meta[:, 2:3].astype(F32)
    total = tally = 0.0
    for beside in range(3):
        ids = rows[2 * beside : 2 * beside + 1, 0:count]
        ratio = rows[2 * beside : 2 * beside + 1, count : 2 * count]
        ratio = ratio + rows[2 * beside + 1 : 2 * beside + 2, 0:count]
        ratio = ratio + rows[2 * beside + 1 : 2 * beside + 2, count : 2 * count]
        same = (own_id == ids).astype(F32)
        tally = tally + jnp.sum(same, axis=1, keepdims=True)
        total = total + jnp.sum(same * ratio, axis=1, keepdims=True)
    own = meta[:, 12:13].astype(F32) + meta[:, 13:14].astype(F32) + meta[:, 14:15].astype(F32)
    return own * jnp.minimum(jnp.exp(total / tally), CLIP_HIGH)


def hold_kernel(rows, earlier, out):
    del earlier
    out[...] = rows[...]


def cut_of(offset, width):
    return pl.multiple_of((lax.axis_index("tp") + offset + CUTS) % CUTS * width, width)


def forward_kernel(
    x0, xm1, xp1, x2, near, group, w_gate, w_up, w_down,
    y0, ym1, yp1, y2, gate_out, up_out, weights,
):
    width = x0.shape[1]
    weight = sequence_weights(near, group[:, group.shape[1] - META :])
    weights[...] = jnp.broadcast_to(weight, weights.shape)
    gate_pre = up_pre = 0.0
    for rows, offset in ((x0, 0), (xm1, -1), (xp1, 1), (x2, 2)):
        cut = pl.ds(cut_of(offset, width), width)
        gate_pre += jnp.dot(rows[...], w_gate[cut, :], preferred_element_type=F32)
        up_pre += jnp.dot(rows[...], w_up[cut, :], preferred_element_type=F32)
    gate_out[...] = gate_pre
    up_out[...] = up_pre
    hidden = (gate_pre * jax.nn.sigmoid(gate_pre) * up_pre).astype(BF16)
    for rows, offset in ((y2, 2), (yp1, 1), (ym1, -1), (y0, 0)):
        cut = pl.ds(cut_of(offset, width), width)
        rows[...] = jnp.dot(hidden, w_down[:, cut], preferred_element_type=F32).astype(BF16)


CONTRACT_LAST = (((1,), (1,)), ((), ()))


def input_grad(d_gate, d_up, w_gate, w_up, cut):
    total = lax.dot_general(d_gate, w_gate[cut, :], CONTRACT_LAST, preferred_element_type=F32)
    total += lax.dot_general(d_up, w_up[cut, :], CONTRACT_LAST, preferred_element_type=F32)
    return total.astype(BF16)


def backward_kernel(d0, dm1, dp1, d2, gate, up, w_gate, w_up, w_down, g2, gate_out, up_out):
    width = d0.shape[1]
    d_hidden = 0.0
    for rows, offset in ((d0, 0), (dm1, -1), (dp1, 1), (d2, 2)):
        cut = pl.ds(cut_of(offset, width), width)
        d_hidden += lax.dot_general(
            rows[...], w_down[:, cut], CONTRACT_LAST, preferred_element_type=F32
        )
    gate_pre = gate[...]
    squash = jax.nn.sigmoid(gate_pre)
    d_gate = (d_hidden * up[...] * squash * (1.0 + gate_pre * (1.0 - squash))).astype(BF16)
    d_up = (d_hidden * (gate_pre * squash)).astype(BF16)
    gate_out[...] = d_gate
    up_out[...] = d_up
    g2[...] = input_grad(d_gate, d_up, w_gate, w_up, pl.ds(cut_of(2, width), width))


def rest_kernel(d_gate, d_up, w_gate, w_up, g0, gm1, gp1):
    width = g0.shape[1]
    for rows, offset in ((gm1, -1), (gp1, 1), (g0, 0)):
        cut = pl.ds(cut_of(offset, width), width)
        rows[...] = input_grad(d_gate[...], d_up[...], w_gate, w_up, cut)


def sum_kernel(y0, g0, left, y_right, g_right, out):
    slots, width = y0.shape
    shape = (out.shape[0], out.shape[1], width)
    for own, right, half in ((y0, y_right, 0), (g0, g_right, 1)):
        total = own[...].astype(F32) + right[...].astype(F32)
        total = total + left[half * slots : (half + 1) * slots, :].astype(F32)
        out[:, :, half * width : (half + 1) * width] = total.astype(BF16).reshape(shape)


def combine_kernel(back, group, weights, hots, out):
    slots, both = back.shape[0] * back.shape[1], back.shape[2]
    width = both // 2
    count = group.shape[0]
    returned = back[...].reshape(slots, both)
    meta = group[:, both : both + META].astype(F32)
    weight = weights[:, 0:1]
    upstream = group[:, width:both].astype(F32)
    total = 0.0
    columns = []
    for k in range(2):
        picked = jnp.dot(hots[k], returned, preferred_element_type=F32)
        first = 6 + 3 * k
        gate = meta[:, first : first + 1] + meta[:, first + 1 : first + 2]
        gate = gate + meta[:, first + 2 : first + 3]
        total = total + gate * picked
        term = weight * jnp.sum(upstream * picked[:, 0:width], axis=1, keepdims=True)
        columns += list(split3(term))
    out[:, 0:width] = total[:, 0:width].astype(BF16)
    out[:, width:both] = (weight * total[:, width:both]).astype(BF16)
    out[:, both : both + META] = lanes(count, columns).astype(BF16)


def unpack_kernel(arrived, mixed, grad_tokens, grad_gates):
    parts, rows = arrived.shape[0], arrived.shape[1]
    width = mixed.shape[1] // CUTS
    terms = jnp.zeros((rows, META), F32)
    for t in range(parts):
        terms += arrived[t, :, 2 * width : 2 * width + META].astype(F32)
    for q in range(CUTS):
        total = 0.0
        for t in range(q, parts, CUTS):
            total = total + arrived[t, :, 0 : 2 * width].astype(F32)
        cut = slice(q * width, (q + 1) * width)
        mixed[:, cut] = total[:, 0:width].astype(BF16)
        grad_tokens[:, cut] = total[:, width : 2 * width].astype(BF16)
    for k in range(2):
        column = (
            terms[:, 3 * k : 3 * k + 1]
            + terms[:, 3 * k + 1 : 3 * k + 2]
            + terms[:, 3 * k + 2 : 3 * k + 3]
        )
        grad_gates[k : k + 1, :] = row_of(column, rows)


def call(kernel, shapes, *operands, mib=8):
    return pl.pallas_call(
        kernel,
        out_shape=shapes,
        cost_estimate=pl.CostEstimate(flops=0, bytes_accessed=0, transcendentals=0),
        compiler_params=pltpu.CompilerParams(vmem_limit_bytes=mib * 1024 * 1024),
    )(*operands)


def struct(*shape, dtype=BF16):
    return jax.ShapeDtypeStruct(shape, dtype)


def shift(rows, places):
    size = lax.axis_size("tp")
    return lax.ppermute(rows, "tp", [(i, (i + places) % size) for i in range(size)])


def add(left, right):
    return (left.astype(F32) + right.astype(F32)).astype(BF16)


def per_device(
    tokens, routes, gate_weights, seq_ids, log_ratio, advantage, upstream, w_gate, w_up, w_down
):
    count, model = tokens.shape
    parts = lax.axis_size("tp")
    groups = lax.axis_size("dp") * lax.axis_size("ctx")
    group_tokens = count * parts
    width = model // CUTS
    both = 2 * width
    slots = 2 * groups
    gate_local, up_local, down_local = w_gate[0], w_up[0], w_down[0]

    packed = call(
        pack_kernel,
        struct(parts, count, both + META),
        tokens,
        upstream,
        routes.T,
        gate_weights.T,
        seq_ids.reshape(1, count),
        log_ratio.reshape(1, count),
        advantage.reshape(1, -1),
        mib=PACK_MIB,
    )
    group = lax.all_to_all(packed, "tp", 0, 0).reshape(group_tokens, both + META)
    sent, hots = call(
        dispatch_kernel,
        (struct(groups, 2, both + META), struct(2, group_tokens, slots)),
        group,
    )
    arrived = lax.all_to_all(sent, GROUP_AXES, 0, 0)
    x0, d0, near = call(
        arrive_kernel, (struct(slots, width), struct(slots, width), struct(slots, META)), arrived
    )
    xm1, dp1 = shift(x0, 1), shift(d0, -1)
    xp1 = shift(x0, -1)
    x2, d2 = shift(xm1, 1), shift(dp1, -1)
    dm1 = shift(call(hold_kernel, struct(slots, width), d0, dp1), 1)

    piece = struct(slots, width)
    inner = struct(slots, gate_local.shape[1], dtype=F32)
    y0, ym1, yp1, y2, gate_pre, up_pre, weights = call(
        forward_kernel,
        (piece,) * 4 + (inner,) * 2 + (struct(group_tokens, META, dtype=F32),),
        x0, xm1, xp1, x2, near, group, gate_local, up_local, down_local,
        mib=16,
    )
    slope = struct(slots, gate_local.shape[1])
    g2, d_gate, d_up = call(
        backward_kernel,
        (piece, slope, slope),
        d0, dm1, dp1, d2, gate_pre, up_pre, gate_local, up_local, down_local,
        mib=16,
    )
    g0, gm1, gp1 = call(
        rest_kernel, (piece,) * 3, d_gate, d_up, gate_local, up_local, mib=16
    )
    y_far, y_right, g_far = shift(y2, -1), shift(yp1, 1), shift(g2, 1)
    left = shift(jnp.concatenate([add(ym1, y_far), gm1], axis=0), -1)
    g_right = shift(add(gp1, g_far), 1)
    summed = call(sum_kernel, struct(groups, 2, both), y0, g0, left, y_right, g_right)

    back = lax.all_to_all(summed, GROUP_AXES, 0, 0)
    combined = call(
        combine_kernel,
        struct(group_tokens, both + META),
        back,
        group,
        weights,
        hots,
    )
    home = lax.all_to_all(combined.reshape(parts, count, both + META), "tp", 0, 0)
    mixed, grad_tokens, grad_gates = call(
        unpack_kernel,
        (struct(count, model), struct(count, model), struct(2, count, dtype=F32)),
        home,
    )
    return mixed, grad_tokens, grad_gates.T


def solution(mesh):
    rows = ("dp", "ctx", "tp")
    in_specs = (
        P(rows, None),
        P(rows, None),
        P(rows, None),
        P(rows),
        P(rows),
        P(),
        P(rows, None),
        P(GROUP_AXES, None, "tp"),
        P(GROUP_AXES, None, "tp"),
        P(GROUP_AXES, "tp", None),
    )
    out_specs = (P(rows, None), P(rows, None), P(rows, None))
    return jax.shard_map(
        per_device, mesh=mesh, in_specs=in_specs, out_specs=out_specs, check_vma=False
    )
```
